32 devices in a mesh: row: 8 (over y, x, core), col: 4 (over z).
Axes of the slice: x: 2, y: 2, z: 4, core: 2. Of those that a mesh axis runs over, the one named last changes fastest.
Arguments:
- efield_x: float32 [32, 32, 512], P('row', 'col'), may hold values from -0.6 to 0.6
- efield_y: float32 [32, 32, 512], P('row', 'col'), may hold values from -0.6 to 0.6
- efield_z: float32 [32, 32, 512], P('row', 'col'), may hold values from -0.6 to 0.6
- hfield_x: float32 [32, 32, 512], P('row', 'col'), may hold values from -0.6 to 0.6
- hfield_y: float32 [32, 32, 512], P('row', 'col'), may hold values from -0.6 to 0.6
- hfield_z: float32 [32, 32, 512], P('row', 'col'), may hold values from -0.6 to 0.6
- permittivity: float32 [32, 32, 512], P('row', 'col'), may hold values from 1 to 4.4
- conductivity: float32 [32, 32, 512], P('row', 'col'), may hold values from 0.001 to 0.05
Outputs:
- next_ex: float32 [32, 32, 512], P('row', 'col')
- next_ey: float32 [32, 32, 512], P('row', 'col')
- next_ez: float32 [32, 32, 512], P('row', 'col')
- next_hx: float32 [32, 32, 512], P('row', 'col')
- next_hy: float32 [32, 32, 512], P('row', 'col')
- next_hz: float32 [32, 32, 512], P('row', 'col')
The draws below stay inside these ranges and needn't reach their ends.
All inputs are finite; a program needn't handle non-finite values.
Results may differ from the reference program's by a relative error of at most 0.0055.
Values sent between devices are 32-bit elements; how exact they have to be, the bound alone decides.
A program may use at most 64 MiB of HBM per device.

```python
import math
import jax
import jax.numpy as jnp
from jax import lax

NX = 512
NY = 32
NZ = 32


def shard_levels(rng, dims, pieces, smallest, top_value):
    def one(position, parts):
        draws = jax.random.uniform(jax.random.fold_in(jax.random.fold_in(rng, 6), position), (parts,), jnp.float32, smallest / len(pieces), top_value / len(pieces))
        return jnp.repeat(jnp.exp(draws), dims[position] // parts).reshape((-1,) + (1,) * (len(dims) - position - 1))

    factor_of = one(*pieces[0])
    for cut in pieces[1:]:
        factor_of = factor_of * one(*cut)
    return factor_of


def centred(rng, shape, width, reach, shards=(), held_as=jnp.bfloat16):
    array = jax.random.normal(rng, shape, jnp.float32) * width
    if len(shards) > 0:
        array = shard_levels(rng, shape, shards, -0.22, 0.18) * array
    return jnp.clip(array, min=-reach, max=reach).astype(held_as)


def setup_inputs(seed: int = 0) -> dict:
    key_list = jax.random.split(jax.random.key(seed), 9)
    return {
        "efield_x": centred(key_list[0], (NY, NZ, NX), 0.1, 0.6, ((0, 8), (1, 4)), jnp.float32),
        "efield_y": centred(key_list[1], (NY, NZ, NX), 0.1, 0.6, ((0, 8), (1, 4)), jnp.float32),
        "efield_z": centred(key_list[2], (NY, NZ, NX), 0.1, 0.6, ((0, 8), (1, 4)), jnp.float32),
        "hfield_x": centred(key_list[3], (NY, NZ, NX), 0.1, 0.6, ((0, 8), (1, 4)), jnp.float32),
        "hfield_y": centred(key_list[4], (NY, NZ, NX), 0.1, 0.6, ((0, 8), (1, 4)), jnp.float32),
        "hfield_z": centred(key_list[5], (NY, NZ, NX), 0.1, 0.6, ((0, 8), (1, 4)), jnp.float32),
        "permittivity": jnp.clip(jnp.exp(math.log(4.4) - 1.4816046 * jax.random.uniform(key_list[6], (NY, NZ, NX), jnp.float32) ** shard_levels(key_list[6], (NY, NZ, NX), ((0, 8), (1, 4)), -0.2, 0.2)), 1.0, 4.4),
        "conductivity": jnp.clip(jnp.exp(math.log(0.05) - 3.912023 * jax.random.uniform(key_list[7], (NY, NZ, NX), jnp.float32) ** shard_levels(key_list[7], (NY, NZ, NX), ((0, 8), (1, 4)), -0.2, 0.2)), 0.001, 0.05),
    }


HALF_STEP = 30.0


def shifted(values, stride, line_axis, filler, forward):
    length = values.shape[line_axis]
    padding = jnp.full_like(lax.slice_in_dim(values, 0, stride, axis=line_axis), filler)
    if forward:
        return jnp.concatenate([lax.slice_in_dim(values, stride, length, axis=line_axis), padding], line_axis)
    return jnp.concatenate([padding, lax.slice_in_dim(values, 0, length - stride, axis=line_axis)], line_axis)


def diff_up(values, line_axis):
    return shifted(values, 1, line_axis, 0.0, True) - values


def diff_down(values, line_axis):
    return values - shifted(values, 1, line_axis, 0.0, False)


def reduce_lines(sub_diag, main_diag, super_diag, source, line_axis):
    length = source.shape[line_axis]
    stride = 1
    while stride < length:
        sub_lo = shifted(sub_diag, stride, line_axis, 0.0, False)
        mid_lo = shifted(main_diag, stride, line_axis, 1.0, False)
        sup_lo = shifted(super_diag, stride, line_axis, 0.0, False)
        src_lo = shifted(source, stride, line_axis, 0.0, False)
        sub_hi = shifted(sub_diag, stride, line_axis, 0.0, True)
        mid_hi = shifted(main_diag, stride, line_axis, 1.0, True)
        sup_hi = shifted(super_diag, stride, line_axis, 0.0, True)
        src_hi = shifted(source, stride, line_axis, 0.0, True)
        ratio_lo = sub_diag / mid_lo
        ratio_hi = super_diag / mid_hi
        sub_diag = -sub_lo * ratio_lo
        super_diag = -sup_hi * ratio_hi
        main_diag = main_diag - sup_lo * ratio_lo - sub_hi * ratio_hi
        source = source - src_lo * ratio_lo - src_hi * ratio_hi
        stride = stride * 2
    return source / main_diag


def line_flags(length, line_axis, rank):
    iota_shape = [1] * rank
    iota_shape[line_axis] = length
    where_line = lax.broadcasted_iota(jnp.int32, tuple(iota_shape), line_axis)
    return where_line == 0, where_line == length - 1


def line_system(coupling, is_first, is_final):
    sub_diag = jnp.where(is_first, 0.0, -coupling)
    main_diag = jnp.where(is_first, 1.0 + coupling, 1.0 + 2.0 * coupling)
    super_diag = jnp.where(is_final, 0.0, -coupling)
    return sub_diag, main_diag, super_diag


def solve_local(source, coupling, line_axis):
    is_first, is_final = line_flags(source.shape[line_axis], line_axis, source.ndim)
    sub_diag, main_diag, super_diag = line_system(coupling, is_first, is_final)
    return reduce_lines(sub_diag, main_diag, super_diag, source, line_axis)


def reference(efield_x, efield_y, efield_z, hfield_x, hfield_y, hfield_z, permittivity, conductivity):
    damping = conductivity * HALF_STEP / (2.0 * permittivity)
    keep_coef = (1.0 - damping) / (1.0 + damping)
    drive_coef = HALF_STEP / (permittivity * (1.0 + damping))
    coupling = drive_coef * HALF_STEP
    source_x = keep_coef * efield_x + drive_coef * (diff_down(hfield_z, 0) - diff_down(hfield_y, 1) - HALF_STEP * diff_down(diff_up(efield_y, 2), 0))
    source_y = keep_coef * efield_y + drive_coef * (diff_down(hfield_x, 1) - diff_down(hfield_z, 2) - HALF_STEP * diff_down(diff_up(efield_z, 0), 1))
    source_z = keep_coef * efield_z + drive_coef * (diff_down(hfield_y, 2) - diff_down(hfield_x, 0) - HALF_STEP * diff_down(diff_up(efield_x, 1), 2))
    half_ex = solve_local(source_x, coupling, 0)
    half_ey = solve_local(source_y, coupling, 1)
    half_ez = solve_local(source_z, coupling, 2)
    half_hx = hfield_x + HALF_STEP * (diff_up(half_ey, 1) - diff_up(efield_z, 0))
    half_hy = hfield_y + HALF_STEP * (diff_up(half_ez, 2) - diff_up(efield_x, 1))
    half_hz = hfield_z + HALF_STEP * (diff_up(half_ex, 0) - diff_up(efield_y, 2))
    second_x = keep_coef * half_ex + drive_coef * (diff_down(half_hz, 0) - diff_down(half_hy, 1) - HALF_STEP * diff_down(diff_up(half_ez, 2), 1))
    second_y = keep_coef * half_ey + drive_coef * (diff_down(half_hx, 1) - diff_down(half_hz, 2) - HALF_STEP * diff_down(diff_up(half_ex, 0), 2))
    second_z = keep_coef * half_ez + drive_coef * (diff_down(half_hy, 2) - diff_down(half_hx, 0) - HALF_STEP * diff_down(diff_up(half_ey, 1), 0))
    next_ex = solve_local(second_x, coupling, 1)
    next_ey = solve_local(second_y, coupling, 2)
    next_ez = solve_local(second_z, coupling, 0)
    next_hx = half_hx + HALF_STEP * (diff_up(half_ey, 1) - diff_up(next_ez, 0))
    next_hy = half_hy + HALF_STEP * (diff_up(half_ez, 2) - diff_up(next_ex, 1))
    next_hz = half_hz + HALF_STEP * (diff_up(half_ex, 0) - diff_up(next_ey, 2))
    return (next_ex, next_ey, next_ez, next_hx, next_hy, next_hz)
```

```python
import functools

import jax
import jax.numpy as jnp
from jax import lax
from jax.experimental import pallas as pl
from jax.experimental.pallas import tpu as pltpu
from jax.sharding import PartitionSpec as P

STEP = 30.0
MESH = pl.DeviceIdType.MESH
SIDE = 15.0
AREA = 900.0


def roll_to(values, stride, axis):
    return pltpu.roll(values, stride % values.shape[axis], axis)


def edge(shape, axis, where_at):
    return lax.broadcasted_iota(jnp.int32, shape, axis) == where_at


def up_x(values):
    last = edge(values.shape, 2, values.shape[2] - 1)
    return jnp.where(last, 0.0, roll_to(values, -1, 2)) - values


def down_x(values):
    return values - jnp.where(edge(values.shape, 2, 0), 0.0, roll_to(values, 1, 2))


def up_z(values, above):
    last = edge(values.shape, 1, values.shape[1] - 1)
    return jnp.where(last, above, roll_to(values, -1, 1)) - values


def down_z(values, below):
    return values - jnp.where(edge(values.shape, 1, 0), below, roll_to(values, 1, 1))


def up_y(values, above):
    return jnp.concatenate([values[1:], above], 0) - values


def down_y(values, below):
    return values - jnp.concatenate([below, values[:-1]], 0)


def levels_of(length):
    strides = []
    while (1 << len(strides)) < length:
        strides.append(1 << len(strides))
    return strides


def chain_factors(link, excess, axis, keep):
    for level, stride in enumerate(levels_of(link.shape[axis])):
        link_hi = roll_to(link, -stride, axis)
        inverse = 1.0 / (link + link_hi + excess)
        ratio_lo = link * roll_to(inverse, stride, axis)
        ratio_hi = roll_to(link * inverse, -stride, axis)
        keep(2 * level, ratio_lo)
        keep(2 * level + 1, ratio_hi)
        excess = (
            excess
            + ratio_lo * roll_to(excess, stride, axis)
            + ratio_hi * roll_to(excess, -stride, axis)
        )
        link = ratio_lo * roll_to(link, stride, axis)
    return 1.0 / excess


def chain_solve(load, inverse, load_source, axis):
    source = load_source
    for level, stride in enumerate(levels_of(source.shape[axis])):
        source = (
            source
            + load(2 * level) * roll_to(source, stride, axis)
            + load(2 * level + 1) * roll_to(source, -stride, axis)
        )
    return source * inverse


def kernel(
    rows, cols,
    ex, ey, ez, hx, hy, hz, eps, sig,
    o_ex, o_ey, o_ez, o_hx, o_hy, o_hz,
    y_mat, z_mat, y_mat_in, z_mat_in,
    y_src, z_src, y_src_in, z_src_in,
    y_out, z_out, y_back, z_back,
    face_z, halo_y, halo_z,
    y_alpha, y_beta, z_alpha, z_beta, z_fwd, z_bwd,
    x_fac, y_fac, z_fac,
    halo_sems, row_send, row_recv, col_send, col_recv,
):
    ny, nz, nx = ex.shape
    r = lax.axis_index("row")
    c = lax.axis_index("col")
    zero_y = jnp.zeros(halo_y.shape, jnp.float32)
    zero_z = jnp.zeros(halo_z.shape, jnp.float32)
    halo_y[...] = zero_y
    halo_z[...] = zero_z
    barrier = pltpu.get_barrier_semaphore()
    for d in range(1, rows):
        pl.semaphore_signal(
            barrier, inc=1, device_id=(lax.rem(r + d, rows), c), device_id_type=MESH
        )
    for d in range(1, cols):
        pl.semaphore_signal(
            barrier, inc=1, device_id=(r, lax.rem(c + d, cols)), device_id_type=MESH
        )

    def halo(number, source, target, device):
        return pltpu.make_async_remote_copy(
            src_ref=source, dst_ref=target,
            send_sem=halo_sems.at[0, number], recv_sem=halo_sems.at[1, number],
            device_id=device, device_id_type=MESH,
        )

    face_z[0] = ex[:, 0:1, :]
    face_z[1] = hy[:, nz - 1 : nz, :]
    low_r, high_r = jnp.maximum(r - 1, 0), jnp.minimum(r + 1, rows - 1)
    low_c, high_c = jnp.maximum(c - 1, 0), jnp.minimum(c + 1, cols - 1)
    halos = [
        (r > 0, r < rows - 1, halo(0, ez.at[0], halo_y.at[0], (low_r, c))),
        (c < cols - 1, c > 0, halo(1, face_z.at[1], halo_z.at[1], (r, high_c))),
        (r < rows - 1, r > 0, halo(2, hx.at[ny - 1], halo_y.at[1], (high_r, c))),
        (c > 0, c < cols - 1, halo(3, face_z.at[0], halo_z.at[0], (r, low_c))),
    ]

    def start_halos():
        for target, _, copy in halos:
            pl.when(target)(copy.start)

    def wait_halo(number):
        target, sender, copy = halos[number]
        pl.when(sender)(copy.wait_recv)

    sent = []

    def exchange(step, axis, source, target):
        if axis == "row":
            count, me, send, recv = rows, r, row_send, row_recv
        else:
            count, me, send, recv = cols, c, col_send, col_recv
        copies = []
        for d in range(1, count):
            peer = lax.rem(me + d, count)
            copies.append(
                pltpu.make_async_remote_copy(
                    src_ref=source.at[peer], dst_ref=target.at[me],
                    send_sem=send.at[step, d - 1], recv_sem=recv.at[step, d - 1],
                    device_id=(peer, c) if axis == "row" else (r, peer),
                    device_id_type=MESH,
                )
            )
        for copy in copies:
            copy.start()
        target[me] = source[me]
        sent.extend(copies)
        return copies

    def arrive(copies):
        for copy in copies:
            copy.wait_recv()

    pl.semaphore_wait(barrier, rows - 1 + cols - 1)
    start_halos()

    ground = (eps[...] + SIDE * sig[...]) * (1.0 / AREA)
    link = jnp.ones((nz, nx), jnp.float32)
    left = ground[0]
    carry = ground[1] * 0.0
    for j in range(1, ny):
        here = ground[j] + carry
        beta = 1.0 / (link + 1.0 + here)
        alpha = link * beta
        y_alpha[j] = alpha
        y_beta[j] = beta
        left = left + alpha * here
        carry = beta * here
        link = alpha
    for p in range(rows):
        y_mat[p, 0:1, :] = link[p : p + 1]
        y_mat[p, 1:2, :] = left[p : p + 1]
        y_mat[p, 2:3, :] = carry[p : p + 1]
    y_mat_copies = exchange(0, "row", y_mat, y_mat_in)

    spot = lax.broadcasted_iota(jnp.int32, (ny, nz, nx), 1)
    here = ground
    link = jnp.ones((ny, nz, nx), jnp.float32)
    beta = jnp.ones((ny, nz, nx), jnp.float32)
    for j in range(1, nz):
        flow = beta * here if j > 1 else jnp.zeros_like(here)
        fresh_link = link if j == 1 else roll_to(link * beta, 1, 1)
        fresh = ground + roll_to(flow, 1, 1)
        here = jnp.where(spot == j, fresh, here)
        link = jnp.where(spot == j, fresh_link, link)
        beta = jnp.where(spot == j, 1.0 / (link + 1.0 + here), beta)
    first = spot == 0
    beta = jnp.where(first, 0.0, beta)
    alpha = link * beta
    z_alpha[...] = alpha
    z_beta[...] = beta
    left = jnp.sum(jnp.where(first, ground, alpha * here), axis=1)
    tail = beta * here
    for p in range(cols):
        z_mat[p, 0:1, :] = alpha[p, nz - 1 :, :]
        z_mat[p, 1:2, :] = left[p : p + 1]
        z_mat[p, 2:3, :] = tail[p, nz - 1 :, :]
    z_mat_copies = exchange(0, "col", z_mat, z_mat_in)
    forward = jnp.where(first, 0.0, roll_to(beta, 1, 1))
    backward = jnp.where(spot == nz - 1, 0.0, beta)
    for level, stride in enumerate(levels_of(nz)):
        z_fwd[level] = forward
        z_bwd[level] = backward
        forward = forward * jnp.where(spot < stride, 0.0, roll_to(forward, stride, 1))
        backward = backward * jnp.where(
            spot >= nz - stride, 0.0, roll_to(backward, -stride, 1)
        )

    def reduce_y(body, flux):
        charge = []
        left = body[0] + flux[0]
        for j in range(1, ny):
            now = body[j] + flux[j] - flux[j - 1]
            if j > 1:
                now = now + y_beta[j - 1] * charge[-1]
            charge.append(now)
            left = left + y_alpha[j] * now
        right = y_beta[ny - 1] * charge[-1] - flux[ny - 1]
        return charge, left, right

    def send_y(stage, left, right):
        for p in range(rows):
            y_src[stage, p, 0:1, :] = left[p : p + 1]
            y_src[stage, p, 1:2, :] = right[p : p + 1]
        return exchange(1 + 2 * stage, "row", y_src.at[stage], y_src_in.at[stage])

    def expand_y(stage, charge):
        near = jnp.concatenate([y_back[stage, p, 0:1, :] for p in range(rows)], 0)
        beyond = jnp.concatenate([y_back[stage, p, 1:2, :] for p in range(rows)], 0)
        cells = []
        after = beyond
        for j in range(ny - 1, 0, -1):
            after = y_alpha[j] * near + y_beta[j] * (after + charge[j - 1])
            cells.insert(0, after)
        return jnp.stack([near] + cells, 0), beyond[None]

    def reduce_z(body, flux):
        source = body + flux - jnp.where(first, 0.0, roll_to(flux, 1, 1))
        charge = jnp.where(first, 0.0, source)
        for level, stride in enumerate(levels_of(nz)):
            charge = charge + z_fwd[level] * roll_to(charge, stride, 1)
        left = jnp.sum(jnp.where(first, source, z_alpha[...] * charge), axis=1)
        right = z_beta[...] * charge - flux
        return charge, left, right

    def send_z(stage, left, right):
        for p in range(cols):
            z_src[stage, p, 0:1, :] = left[p : p + 1]
            z_src[stage, p, 1:2, :] = right[p, nz - 1 :, :]
        return exchange(1 + 2 * stage, "col", z_src.at[stage], z_src_in.at[stage])

    def expand_z(stage, charge):
        near = jnp.stack([z_back[stage, p, 0:1, :] for p in range(cols)], 0)
        beyond = jnp.stack([z_back[stage, p, 1:2, :] for p in range(cols)], 0)
        cells = z_alpha[...] * near + z_beta[...] * charge
        cells = cells + jnp.where(spot == nz - 1, z_beta[...] * beyond, 0.0)
        cells = jnp.where(first, near, cells)
        for level, stride in enumerate(levels_of(nz)):
            cells = cells + z_bwd[level] * roll_to(cells, -stride, 1)
        return cells, beyond

    tall = 8

    def rows_of(buffer, number, count, filler):
        parts = [buffer[p, number : number + 1, :] for p in range(count)]
        if count < tall:
            parts.append(jnp.full((tall - count, nx), filler, jnp.float32))
        return jnp.concatenate(parts, 0)

    def line_factors(buffer, count, keep):
        row = lax.broadcasted_iota(jnp.int32, (tall, nx), 0)
        link = rows_of(buffer, 0, count, 0.0)
        left = rows_of(buffer, 1, count, 1.0)
        right = rows_of(buffer, 2, count, 0.0)
        below = row == 0
        excess = left + jnp.where(below, 0.0, roll_to(right, 1, 0))
        excess = excess + jnp.where(row == count - 1, link, 0.0)
        inner_link = jnp.where(below | (row >= count), 0.0, roll_to(link, 1, 0))
        return chain_factors(inner_link, excess, 0, keep)

    def line_solve(stage, source_in, count, load, inverse, out):
        row = lax.broadcasted_iota(jnp.int32, (tall, nx), 0)
        left = rows_of(source_in.at[stage], 0, count, 0.0)
        right = rows_of(source_in.at[stage], 1, count, 0.0)
        source = left + jnp.where(row == 0, 0.0, roll_to(right, 1, 0))
        source = jnp.where(row < count, source, 0.0)
        near = chain_solve(load, inverse, source, 0)
        for p in range(count):
            out[stage, p, 0:1, :] = near[p : p + 1]
            if p < count - 1:
                out[stage, p, 1:2, :] = near[p + 1 : p + 2]
            else:
                out[stage, p, 1:2, :] = jnp.zeros((1, nx), jnp.float32)

    def keeper(ref):
        def keep(number, values):
            ref[number] = values
        return keep

    def loader(ref):
        def load(number):
            return ref[number]
        return load

    keep_ground = (eps[...] - SIDE * sig[...]) * (1.0 / AREA)
    flux_of_z = hz[...] * (1.0 / STEP) - up_x(ey[...])
    wait_halo(1)
    body = keep_ground * ex[...] - down_z(hy[...], halo_z[1]) * (1.0 / STEP)
    y_charge, left, right = reduce_y(body, flux_of_z)
    y_copies = send_y(0, left, right)
    wait_halo(0)
    flux_of_x = hx[...] * (1.0 / STEP) - up_y(ez[...], halo_y[0:1])
    body = keep_ground * ey[...] - down_x(hz[...]) * (1.0 / STEP)
    z_charge, left, right = reduce_z(body, flux_of_x)
    z_copies = send_z(0, left, right)

    arrive(y_mat_copies)
    y_inverse = line_factors(y_mat_in, rows, keeper(y_fac))
    arrive(z_mat_copies)
    z_inverse = line_factors(z_mat_in, cols, keeper(z_fac))

    def half_lines(stage, y_copies, z_copies):
        arrive(y_copies)
        line_solve(stage, y_src_in, rows, loader(y_fac), y_inverse, y_out)
        y_returns = exchange(2 + 2 * stage, "row", y_out.at[stage], y_back.at[stage])
        arrive(z_copies)
        line_solve(stage, z_src_in, cols, loader(z_fac), z_inverse, z_out)
        z_returns = exchange(2 + 2 * stage, "col", z_out.at[stage], z_back.at[stage])
        return y_returns, z_returns

    y_returns, z_returns = half_lines(0, y_copies, z_copies)

    first_x = lax.broadcasted_iota(jnp.int32, (ny, nz, nx), 2) == 0
    last_x = lax.broadcasted_iota(jnp.int32, (ny, nz, nx), 2) == nx - 1
    x_inverse = chain_factors(
        jnp.where(first_x, 0.0, 1.0), ground + jnp.where(last_x, 1.0, 0.0), 2, keeper(x_fac)
    )
    wait_halo(2)
    wait_halo(3)
    flux_of_y = hy[...] * (1.0 / STEP) - up_z(ex[...], halo_z[0])
    body = keep_ground * ez[...] - down_y(hx[...], halo_y[1:2]) * (1.0 / STEP)
    half_ez = chain_solve(loader(x_fac), x_inverse, body + down_x(flux_of_y), 2)
    slope_ez = up_x(half_ez)

    arrive(y_returns)
    half_ex, beyond_ex = expand_y(0, y_charge)
    slope_ex = up_y(half_ex, beyond_ex)
    arrive(z_returns)
    half_ey, beyond_ey = expand_z(0, z_charge)
    slope_ey = up_z(half_ey, beyond_ey)

    lossless = eps[...] * (1.0 / AREA)
    lossy = sig[...] * (SIDE / AREA)
    y_charge, left, right = reduce_y(lossless * half_ez + lossy * ez[...], -slope_ey)
    y_copies = send_y(1, left, right)
    z_charge, left, right = reduce_z(lossless * half_ex + lossy * ex[...], -slope_ez)
    z_copies = send_z(1, left, right)
    y_returns, z_returns = half_lines(1, y_copies, z_copies)

    body = lossless * half_ey + lossy * ey[...]
    mean_ey = chain_solve(loader(x_fac), x_inverse, body - down_x(slope_ex), 2)
    next_ey = 2.0 * mean_ey - ey[...]
    o_ey[...] = next_ey
    o_hz[...] = STEP * (flux_of_z + 2.0 * slope_ex - up_x(next_ey))

    arrive(y_returns)
    mean_ez, beyond_ez = expand_y(1, y_charge)
    next_ez = 2.0 * mean_ez - ez[...]
    o_ez[...] = next_ez
    above = 2.0 * beyond_ez - halo_y[0:1]
    o_hx[...] = STEP * (flux_of_x + 2.0 * slope_ey - up_y(next_ez, above))
    arrive(z_returns)
    mean_ex, beyond_ex = expand_z(1, z_charge)
    next_ex = 2.0 * mean_ex - ex[...]
    o_ex[...] = next_ex
    above = 2.0 * beyond_ex - halo_z[0]
    o_hy[...] = STEP * (flux_of_y + 2.0 * slope_ez - up_z(next_ex, above))

    for target, _, copy in halos:
        pl.when(target)(copy.wait_send)
    for copy in sent:
        copy.wait_send()


def fused(rows, cols, *fields):
    ny, nz, nx = fields[0].shape
    f32 = jnp.float32
    block = (ny, nz, nx)
    y_levels, z_levels = len(levels_of(8)), len(levels_of(8))
    scratch = [
        (rows, 3, nx), (cols, 3, nx), (rows, 3, nx), (cols, 3, nx),
        (2, rows, 2, nx), (2, cols, 2, nx), (2, rows, 2, nx), (2, cols, 2, nx),
        (2, rows, 2, nx), (2, cols, 2, nx), (2, rows, 2, nx), (2, cols, 2, nx),
        (2, ny, 1, nx), (2, nz, nx), (2, ny, 1, nx),
        block, block, block, block,
        (len(levels_of(nz)),) + block, (len(levels_of(nz)),) + block,
        (2 * len(levels_of(nx)),) + block, (2 * y_levels, 8, nx), (2 * z_levels, 8, nx),
    ]
    return pl.pallas_call(
        functools.partial(kernel, rows, cols),
        out_shape=[jax.ShapeDtypeStruct(block, f32)] * 6,
        in_specs=[pl.BlockSpec(memory_space=pltpu.VMEM)] * 8,
        out_specs=[pl.BlockSpec(memory_space=pltpu.VMEM)] * 6,
        scratch_shapes=[pltpu.VMEM(shape, f32) for shape in scratch]
        + [
            pltpu.SemaphoreType.DMA((2, 4)),
            pltpu.SemaphoreType.DMA((5, rows - 1)),
            pltpu.SemaphoreType.DMA((5, rows - 1)),
            pltpu.SemaphoreType.DMA((5, cols - 1)),
            pltpu.SemaphoreType.DMA((5, cols - 1)),
        ],
        compiler_params=pltpu.CompilerParams(
            collective_id=0, has_side_effects=True, vmem_limit_bytes=40 * 1024 * 1024
        ),
        name="step",
    )(*fields)


HALF_STEP = 30.0


def with_halo(cells, sides, width):
    for axis, dim in sides:
        count = lax.axis_size(axis)
        ends = count - 1
        head = lax.slice_in_dim(cells, 0, width, axis=dim)
        tail = lax.slice_in_dim(cells, cells.shape[dim] - width, cells.shape[dim], axis=dim)
        cells = jnp.concatenate(
            [
                lax.ppermute(tail, axis, [(i, (i + 1) % count) for i in range(ends)]),
                cells,
                lax.ppermute(head, axis, [((i + 1) % count, i) for i in range(ends)]),
            ],
            axis=dim,
        )
    return cells


def shifted(values, stride, line_axis, filler, forward):
    length = values.shape[line_axis]
    padding = jnp.full_like(lax.slice_in_dim(values, 0, stride, axis=line_axis), filler)
    if forward:
        return jnp.concatenate(
            [lax.slice_in_dim(values, stride, length, axis=line_axis), padding], line_axis
        )
    return jnp.concatenate(
        [padding, lax.slice_in_dim(values, 0, length - stride, axis=line_axis)], line_axis
    )


def diff_up(values, line_axis):
    return shifted(values, 1, line_axis, 0.0, True) - values


def diff_down(values, line_axis):
    return values - shifted(values, 1, line_axis, 0.0, False)


def reduce_lines(sub_diag, main_diag, super_diag, source, line_axis):
    length = source.shape[line_axis]
    stride = 1
    while stride < length:
        sub_lo = shifted(sub_diag, stride, line_axis, 0.0, False)
        mid_lo = shifted(main_diag, stride, line_axis, 1.0, False)
        sup_lo = shifted(super_diag, stride, line_axis, 0.0, False)
        src_lo = shifted(source, stride, line_axis, 0.0, False)
        sub_hi = shifted(sub_diag, stride, line_axis, 0.0, True)
        mid_hi = shifted(main_diag, stride, line_axis, 1.0, True)
        sup_hi = shifted(super_diag, stride, line_axis, 0.0, True)
        src_hi = shifted(source, stride, line_axis, 0.0, True)
        ratio_lo = sub_diag / mid_lo
        ratio_hi = super_diag / mid_hi
        sub_diag = -sub_lo * ratio_lo
        super_diag = -sup_hi * ratio_hi
        main_diag = main_diag - sup_lo * ratio_lo - sub_hi * ratio_hi
        source = source - src_lo * ratio_lo - src_hi * ratio_hi
        stride = stride * 2
    return source / main_diag


def line_flags(length, line_axis, rank):
    iota_shape = [1] * rank
    iota_shape[line_axis] = length
    where_line = lax.broadcasted_iota(jnp.int32, tuple(iota_shape), line_axis)
    return (where_line == 0, where_line == length - 1)


def line_system(coupling, is_first, is_final):
    sub_diag = jnp.where(is_first, 0.0, -coupling)
    main_diag = jnp.where(is_first, 1.0 + coupling, 1.0 + 2.0 * coupling)
    super_diag = jnp.where(is_final, 0.0, -coupling)
    return (sub_diag, main_diag, super_diag)


def solve_local(source, coupling, line_axis):
    is_first, is_final = line_flags(source.shape[line_axis], line_axis, source.ndim)
    sub_diag, main_diag, super_diag = line_system(coupling, is_first, is_final)
    return reduce_lines(sub_diag, main_diag, super_diag, source, line_axis)


def inner(values):
    return values[1:-1, 1:-1]


def with_faces(stacked):
    return with_halo(stacked, (("row", 1), ("col", 2)), 1)


def inside_mask(count_y, count_z):
    pos_y = (
        lax.axis_index("row") * count_y
        + lax.broadcasted_iota(jnp.int32, (count_y + 2, 1, 1), 0)
        - 1
    )
    pos_z = (
        lax.axis_index("col") * count_z
        + lax.broadcasted_iota(jnp.int32, (1, count_z + 2, 1), 1)
        - 1
    )
    inside = (
        (pos_y >= 0)
        & (pos_y < count_y * lax.axis_size("row"))
        & (pos_z >= 0)
        & (pos_z < count_z * lax.axis_size("col"))
    )
    return inside.astype(jnp.float32)


def solve_rows_moved(source, coupling):

    def along_lines(pieces):
        moved_source, moved_coupling = pieces
        turned_source = jnp.transpose(moved_source, (1, 2, 0))
        turned_coupling = jnp.transpose(moved_coupling, (1, 2, 0))
        solved = solve_local(turned_source, turned_coupling, 2)
        solved = jnp.transpose(solved, (2, 0, 1))
        return lax.all_to_all(solved, "row", split_axis=0, concat_axis=2, tiled=True)

    return along_lines(
        (
            lax.all_to_all(source, "row", split_axis=2, concat_axis=0, tiled=True),
            lax.all_to_all(coupling, "row", split_axis=2, concat_axis=0, tiled=True),
        )
    )


def solve_rows(source, coupling):
    return solve_rows_moved(source, coupling)


def solve_columns(source, coupling):

    def along_lines(pieces):
        moved_source, moved_coupling = pieces
        solved = solve_local(moved_source, moved_coupling, 1)
        return lax.all_to_all(solved, "col", split_axis=1, concat_axis=2, tiled=True)

    return along_lines(
        (
            lax.all_to_all(source, "col", split_axis=2, concat_axis=1, tiled=True),
            lax.all_to_all(coupling, "col", split_axis=2, concat_axis=1, tiled=True),
        )
    )


def on_device(
    efield_x, efield_y, efield_z, hfield_x, hfield_y, hfield_z, permittivity, conductivity
):
    count_y = efield_x.shape[0]
    count_z = efield_x.shape[1]
    damping = conductivity * HALF_STEP / (2.0 * permittivity)
    keep_coef = (1.0 - damping) / (1.0 + damping)
    drive_coef = HALF_STEP / (permittivity * (1.0 + damping))
    coupling = drive_coef * HALF_STEP
    old_all = with_faces(jnp.stack([efield_x, efield_y, efield_z, hfield_x, hfield_y, hfield_z]))
    old_ex, old_ey, old_ez = (old_all[0], old_all[1], old_all[2])
    old_hx, old_hy, old_hz = (old_all[3], old_all[4], old_all[5])
    source_x = keep_coef * efield_x + drive_coef * (
        inner(diff_down(old_hz, 0))
        - inner(diff_down(old_hy, 1))
        - HALF_STEP * inner(diff_down(diff_up(old_ey, 2), 0))
    )
    source_y = keep_coef * efield_y + drive_coef * (
        inner(diff_down(old_hx, 1))
        - diff_down(hfield_z, 2)
        - HALF_STEP * inner(diff_down(diff_up(old_ez, 0), 1))
    )
    source_z = keep_coef * efield_z + drive_coef * (
        diff_down(hfield_y, 2)
        - inner(diff_down(old_hx, 0))
        - HALF_STEP * inner(diff_down(diff_up(old_ex, 1), 2))
    )
    half_ex = solve_rows(source_x, coupling)
    half_ey = solve_columns(source_y, coupling)
    half_ez = solve_local(source_z, coupling, 2)
    mid_all = with_faces(jnp.stack([half_ex, half_ey, half_ez]))
    mid_ex, mid_ey, mid_ez = (mid_all[0], mid_all[1], mid_all[2])
    inside = inside_mask(count_y, count_z)
    dz_mid_ey = diff_up(mid_ey, 1)
    dx_mid_ez = diff_up(mid_ez, 2)
    dy_mid_ex = diff_up(mid_ex, 0)
    mid_hx = (old_hx + HALF_STEP * (dz_mid_ey - diff_up(old_ez, 0))) * inside
    mid_hy = (old_hy + HALF_STEP * (dx_mid_ez - diff_up(old_ex, 1))) * inside
    mid_hz = (old_hz + HALF_STEP * (dy_mid_ex - diff_up(old_ey, 2))) * inside
    second_x = keep_coef * half_ex + drive_coef * (
        inner(diff_down(mid_hz, 0))
        - inner(diff_down(mid_hy, 1))
        - HALF_STEP * inner(diff_down(dx_mid_ez, 1))
    )
    second_y = keep_coef * half_ey + drive_coef * (
        inner(diff_down(mid_hx, 1))
        - inner(diff_down(mid_hz, 2))
        - HALF_STEP * inner(diff_down(dy_mid_ex, 2))
    )
    second_z = keep_coef * half_ez + drive_coef * (
        inner(diff_down(mid_hy, 2))
        - inner(diff_down(mid_hx, 0))
        - HALF_STEP * inner(diff_down(dz_mid_ey, 0))
    )
    next_ex = solve_columns(second_x, coupling)
    next_ey = solve_local(second_y, coupling, 2)
    next_ez = solve_rows(second_z, coupling)
    last_all = with_faces(jnp.stack([next_ex, next_ez]))
    next_hx = inner(mid_hx) + HALF_STEP * (inner(dz_mid_ey) - inner(diff_up(last_all[1], 0)))
    next_hy = inner(mid_hy) + HALF_STEP * (inner(dx_mid_ez) - inner(diff_up(last_all[0], 1)))
    next_hz = inner(mid_hz) + HALF_STEP * (inner(dy_mid_ex) - diff_up(next_ey, 2))
    return (next_ex, next_ey, next_ez, next_hx, next_hy, next_hz)


def solution(mesh):
    rows, cols = mesh.shape["row"], mesh.shape["col"]
    placed = (
        P("row", "col", None),
        P("row", "col", None),
        P("row", "col", None),
        P("row", "col", None),
        P("row", "col", None),
        P("row", "col", None),
        P("row", "col", None),
        P("row", "col", None),
    )

    def per_device(*fields):
        ny, nz = fields[0].shape[:2]
        if nz == rows == 8 and ny == cols and 1 < cols < 8:
            return tuple(fused(rows, cols, *fields))
        return on_device(*fields)

    return jax.shard_map(
        per_device,
        mesh=mesh,
        in_specs=placed,
        out_specs=(
            P("row", "col", None),
            P("row", "col", None),
            P("row", "col", None),
            P("row", "col", None),
            P("row", "col", None),
            P("row", "col", None),
        ),
        check_vma=False,
    )
```

```python
import functools

import jax
import jax.numpy as jnp
from jax import lax
from jax.experimental import pallas as pl
from jax.experimental.pallas import tpu as pltpu
from jax.sharding import PartitionSpec as P

STEP = 30.0
MESH = pl.DeviceIdType.MESH
SIDE = 15.0
VMEM_LIMIT = 40 * 1024 * 1024
AREA = 900.0


def roll_to(values, stride, axis):
    return pltpu.roll(values, stride % values.shape[axis], axis)


def edge(shape, axis, where_at):
    return lax.broadcasted_iota(jnp.int32, shape, axis) == where_at


def up_x(values):
    last = edge(values.shape, 2, values.shape[2] - 1)
    return jnp.where(last, 0.0, roll_to(values, -1, 2)) - values


def down_x(values):
    return values - jnp.where(edge(values.shape, 2, 0), 0.0, roll_to(values, 1, 2))


def up_z(values, above):
    last = edge(values.shape, 1, values.shape[1] - 1)
    return jnp.where(last, above, roll_to(values, -1, 1)) - values


def down_z(values, below):
    return values - jnp.where(edge(values.shape, 1, 0), below, roll_to(values, 1, 1))


def up_y(values, above):
    return jnp.concatenate([values[1:], above], 0) - values


def down_y(values, below):
    return values - jnp.concatenate([below, values[:-1]], 0)


def levels_of(length):
    strides = []
    while (1 << len(strides)) < length:
        strides.append(1 << len(strides))
    return strides


def chain_factors(link, excess, axis, keep):
    for level, stride in enumerate(levels_of(link.shape[axis])):
        link_hi = roll_to(link, -stride, axis)
        inverse = 1.0 / (link + link_hi + excess)
        ratio_lo = link * roll_to(inverse, stride, axis)
        ratio_hi = roll_to(link * inverse, -stride, axis)
        keep(2 * level, ratio_lo)
        keep(2 * level + 1, ratio_hi)
        excess = (
            excess
            + ratio_lo * roll_to(excess, stride, axis)
            + ratio_hi * roll_to(excess, -stride, axis)
        )
        link = ratio_lo * roll_to(link, stride, axis)
    return 1.0 / excess


def chain_solve(load, inverse, load_source, axis):
    source = load_source
    for level, stride in enumerate(levels_of(source.shape[axis])):
        source = (
            source
            + load(2 * level) * roll_to(source, stride, axis)
            + load(2 * level + 1) * roll_to(source, -stride, axis)
        )
    return source * inverse


def kernel(
    rows, cols,
    *refs,
):
    hbm = refs[:8]
    (
    o_ex, o_ey, o_ez, o_hx, o_hy, o_hz,
    y_mat, z_mat, y_mat_in, z_mat_in,
    y_src, z_src, y_src_in, z_src_in,
    y_out, z_out, y_back, z_back,
    face_z, halo_y, halo_z,
    y_alpha, y_beta, z_alpha, z_beta, z_fwd, z_bwd,
    x_fac, y_fac, z_fac,
    halo_sems, row_send, row_recv, col_send, col_recv,
    fields, field_sems,
    ) = refs[8:]
    ex, ey, ez, hx, hy, hz, eps, sig = [fields.at[i] for i in range(8)]
    loads = [
        pltpu.make_async_copy(hbm[i], fields.at[i], field_sems.at[i]) for i in range(8)
    ]
    for i in (6, 7, 0, 4, 2, 3, 5, 1):
        loads[i].start()
    ny, nz, nx = ex.shape
    r = lax.axis_index("row")
    c = lax.axis_index("col")
    zero_y = jnp.zeros(halo_y.shape, jnp.float32)
    zero_z = jnp.zeros(halo_z.shape, jnp.float32)
    halo_y[...] = zero_y
    halo_z[...] = zero_z
    barrier = pltpu.get_barrier_semaphore()
    for d in range(1, rows):
        pl.semaphore_signal(
            barrier, inc=1, device_id=(lax.rem(r + d, rows), c), device_id_type=MESH
        )
    for d in range(1, cols):
        pl.semaphore_signal(
            barrier, inc=1, device_id=(r, lax.rem(c + d, cols)), device_id_type=MESH
        )

    def halo(number, source, target, device):
        return pltpu.make_async_remote_copy(
            src_ref=source, dst_ref=target,
            send_sem=halo_sems.at[0, number], recv_sem=halo_sems.at[1, number],
            device_id=device, device_id_type=MESH,
        )

    low_r, high_r = jnp.maximum(r - 1, 0), jnp.minimum(r + 1, rows - 1)
    low_c, high_c = jnp.maximum(c - 1, 0), jnp.minimum(c + 1, cols - 1)
    halos = [
        (r > 0, r < rows - 1, halo(0, ez.at[0], halo_y.at[0], (low_r, c))),
        (c < cols - 1, c > 0, halo(1, face_z.at[1], halo_z.at[1], (r, high_c))),
        (r < rows - 1, r > 0, halo(2, hx.at[ny - 1], halo_y.at[1], (high_r, c))),
        (c > 0, c < cols - 1, halo(3, face_z.at[0], halo_z.at[0], (r, low_c))),
    ]

    def start_halos():
        for target, _, copy in halos:
            pl.when(target)(copy.start)

    def wait_halo(number):
        target, sender, copy = halos[number]
        pl.when(sender)(copy.wait_recv)

    sent = []

    def exchange(step, axis, source, target):
        if axis == "row":
            count, me, send, recv = rows, r, row_send, row_recv
        else:
            count, me, send, recv = cols, c, col_send, col_recv
        copies = []
        for d in range(1, count):
            peer = lax.rem(me + d, count)
            copies.append(
                pltpu.make_async_remote_copy(
                    src_ref=source.at[peer], dst_ref=target.at[me],
                    send_sem=send.at[step, d - 1], recv_sem=recv.at[step, d - 1],
                    device_id=(peer, c) if axis == "row" else (r, peer),
                    device_id_type=MESH,
                )
            )
        for copy in copies:
            copy.start()
        target[me] = source[me]
        sent.extend(copies)
        return copies

    def arrive(copies):
        for copy in copies:
            copy.wait_recv()

    loads[6].wait()
    loads[7].wait()
    ground = (eps[...] + SIDE * sig[...]) * (1.0 / AREA)
    link = jnp.ones((nz, nx), jnp.float32)
    left = ground[0]
    carry = ground[1] * 0.0
    for j in range(1, ny):
        here = ground[j] + carry
        beta = 1.0 / (link + 1.0 + here)
        alpha = link * beta
        y_alpha[j] = alpha
        y_beta[j] = beta
        left = left + alpha * here
        carry = beta * here
        link = alpha
    for p in range(rows):
        y_mat[p, 0:1, :] = link[p : p + 1]
        y_mat[p, 1:2, :] = left[p : p + 1]
        y_mat[p, 2:3, :] = carry[p : p + 1]
    for i in (0, 4, 2, 3):
        loads[i].wait()
    face_z[0] = ex[:, 0:1, :]
    face_z[1] = hy[:, nz - 1 : nz, :]
    pl.semaphore_wait(barrier, rows - 1 + cols - 1)
    start_halos()
    y_mat_copies = exchange(0, "row", y_mat, y_mat_in)

    spot = lax.broadcasted_iota(jnp.int32, (ny, nz, nx), 1)
    here = ground
    link = jnp.ones((ny, nz, nx), jnp.float32)
    beta = jnp.ones((ny, nz, nx), jnp.float32)
    for j in range(1, nz):
        flow = beta * here if j > 1 else jnp.zeros_like(here)
        fresh_link = link if j == 1 else roll_to(link * beta, 1, 1)
        fresh = ground + roll_to(flow, 1, 1)
        here = jnp.where(spot == j, fresh, here)
        link = jnp.where(spot == j, fresh_link, link)
        beta = jnp.where(spot == j, 1.0 / (link + 1.0 + here), beta)
    first = spot == 0
    beta = jnp.where(first, 0.0, beta)
    alpha = link * beta
    z_alpha[...] = alpha
    z_beta[...] = beta
    left = jnp.sum(jnp.where(first, ground, alpha * here), axis=1)
    tail = beta * here
    for p in range(cols):
        z_mat[p, 0:1, :] = alpha[p, nz - 1 :, :]
        z_mat[p, 1:2, :] = left[p : p + 1]
        z_mat[p, 2:3, :] = tail[p, nz - 1 :, :]
    z_mat_copies = exchange(0, "col", z_mat, z_mat_in)
    forward = jnp.where(first, 0.0, roll_to(beta, 1, 1))
    backward = jnp.where(spot == nz - 1, 0.0, beta)
    for level, stride in enumerate(levels_of(nz)):
        z_fwd[level] = forward
        z_bwd[level] = backward
        forward = forward * jnp.where(spot < stride, 0.0, roll_to(forward, stride, 1))
        backward = backward * jnp.where(
            spot >= nz - stride, 0.0, roll_to(backward, -stride, 1)
        )

    def reduce_y(body, flux):
        charge = []
        left = body[0] + flux[0]
        for j in range(1, ny):
            now = body[j] + flux[j] - flux[j - 1]
            if j > 1:
                now = now + y_beta[j - 1] * charge[-1]
            charge.append(now)
            left = left + y_alpha[j] * now
        right = y_beta[ny - 1] * charge[-1] - flux[ny - 1]
        return charge, left, right

    def send_y(stage, left, right):
        for p in range(rows):
            y_src[stage, p, 0:1, :] = left[p : p + 1]
            y_src[stage, p, 1:2, :] = right[p : p + 1]
        return exchange(1 + 2 * stage, "row", y_src.at[stage], y_src_in.at[stage])

    def expand_y(stage, charge):
        near = jnp.concatenate([y_back[stage, p, 0:1, :] for p in range(rows)], 0)
        beyond = jnp.concatenate([y_back[stage, p, 1:2, :] for p in range(rows)], 0)
        cells = []
        after = beyond
        for j in range(ny - 1, 0, -1):
            after = y_alpha[j] * near + y_beta[j] * (after + charge[j - 1])
            cells.insert(0, after)
        return jnp.stack([near] + cells, 0), beyond[None]

    def reduce_z(body, flux):
        source = body + flux - jnp.where(first, 0.0, roll_to(flux, 1, 1))
        charge = jnp.where(first, 0.0, source)
        for level, stride in enumerate(levels_of(nz)):
            charge = charge + z_fwd[level] * roll_to(charge, stride, 1)
        left = jnp.sum(jnp.where(first, source, z_alpha[...] * charge), axis=1)
        right = z_beta[...] * charge - flux
        return charge, left, right

    def send_z(stage, left, right):
        for p in range(cols):
            z_src[stage, p, 0:1, :] = left[p : p + 1]
            z_src[stage, p, 1:2, :] = right[p, nz - 1 :, :]
        return exchange(1 + 2 * stage, "col", z_src.at[stage], z_src_in.at[stage])

    def expand_z(stage, charge):
        near = jnp.stack([z_back[stage, p, 0:1, :] for p in range(cols)], 0)
        beyond = jnp.stack([z_back[stage, p, 1:2, :] for p in range(cols)], 0)
        cells = z_alpha[...] * near + z_beta[...] * charge
        cells = cells + jnp.where(spot == nz - 1, z_beta[...] * beyond, 0.0)
        cells = jnp.where(first, near, cells)
        for level, stride in enumerate(levels_of(nz)):
            cells = cells + z_bwd[level] * roll_to(cells, -stride, 1)
        return cells, beyond

    tall = 8

    def rows_of(buffer, number, count, filler):
        parts = [buffer[p, number : number + 1, :] for p in range(count)]
        if count < tall:
            parts.append(jnp.full((tall - count, nx), filler, jnp.float32))
        return jnp.concatenate(parts, 0)

    def line_factors(buffer, count, keep):
        row = lax.broadcasted_iota(jnp.int32, (tall, nx), 0)
        link = rows_of(buffer, 0, count, 0.0)
        left = rows_of(buffer, 1, count, 1.0)
        right = rows_of(buffer, 2, count, 0.0)
        below = row == 0
        excess = left + jnp.where(below, 0.0, roll_to(right, 1, 0))
        excess = excess + jnp.where(row == count - 1, link, 0.0)
        inner_link = jnp.where(below | (row >= count), 0.0, roll_to(link, 1, 0))
        return chain_factors(inner_link, excess, 0, keep)

    def line_solve(stage, source_in, count, load, inverse, out):
        row = lax.broadcasted_iota(jnp.int32, (tall, nx), 0)
        left = rows_of(source_in.at[stage], 0, count, 0.0)
        right = rows_of(source_in.at[stage], 1, count, 0.0)
        source = left + jnp.where(row == 0, 0.0, roll_to(right, 1, 0))
        source = jnp.where(row < count, source, 0.0)
        near = chain_solve(load, inverse, source, 0)
        for p in range(count):
            out[stage, p, 0:1, :] = near[p : p + 1]
            if p < count - 1:
                out[stage, p, 1:2, :] = near[p + 1 : p + 2]
            else:
                out[stage, p, 1:2, :] = jnp.zeros((1, nx), jnp.float32)

    def keeper(ref):
        def keep(number, values):
            ref[number] = values
        return keep

    def loader(ref):
        def load(number):
            return ref[number]
        return load

    first_x = lax.broadcasted_iota(jnp.int32, (ny, nz, nx), 2) == 0
    last_x = lax.broadcasted_iota(jnp.int32, (ny, nz, nx), 2) == nx - 1
    x_inverse = chain_factors(
        jnp.where(first_x, 0.0, 1.0), ground + jnp.where(last_x, 1.0, 0.0), 2, keeper(x_fac)
    )

    loads[5].wait()
    loads[1].wait()
    keep_ground = (eps[...] - SIDE * sig[...]) * (1.0 / AREA)
    flux_of_z = hz[...] * (1.0 / STEP) - up_x(ey[...])
    wait_halo(1)
    body = keep_ground * ex[...] - down_z(hy[...], halo_z[1]) * (1.0 / STEP)
    y_charge, left, right = reduce_y(body, flux_of_z)
    y_copies = send_y(0, left, right)
    wait_halo(0)
    flux_of_x = hx[...] * (1.0 / STEP) - up_y(ez[...], halo_y[0:1])
    body = keep_ground * ey[...] - down_x(hz[...]) * (1.0 / STEP)
    z_charge, left, right = reduce_z(body, flux_of_x)
    z_copies = send_z(0, left, right)

    wait_halo(2)
    wait_halo(3)
    flux_of_y = hy[...] * (1.0 / STEP) - up_z(ex[...], halo_z[0])
    body = keep_ground * ez[...] - down_y(hx[...], halo_y[1:2]) * (1.0 / STEP)
    half_ez = chain_solve(loader(x_fac), x_inverse, body + down_x(flux_of_y), 2)
    slope_ez = up_x(half_ez)

    arrive(y_mat_copies)
    y_inverse = line_factors(y_mat_in, rows, keeper(y_fac))
    arrive(z_mat_copies)
    z_inverse = line_factors(z_mat_in, cols, keeper(z_fac))

    def half_lines(stage, y_copies, z_copies):
        arrive(y_copies)
        line_solve(stage, y_src_in, rows, loader(y_fac), y_inverse, y_out)
        y_returns = exchange(2 + 2 * stage, "row", y_out.at[stage], y_back.at[stage])
        arrive(z_copies)
        line_solve(stage, z_src_in, cols, loader(z_fac), z_inverse, z_out)
        z_returns = exchange(2 + 2 * stage, "col", z_out.at[stage], z_back.at[stage])
        return y_returns, z_returns

    y_returns, z_returns = half_lines(0, y_copies, z_copies)

    arrive(y_returns)
    half_ex, beyond_ex = expand_y(0, y_charge)
    slope_ex = up_y(half_ex, beyond_ex)
    arrive(z_returns)
    half_ey, beyond_ey = expand_z(0, z_charge)
    slope_ey = up_z(half_ey, beyond_ey)

    lossless = eps[...] * (1.0 / AREA)
    lossy = sig[...] * (SIDE / AREA)
    y_charge, left, right = reduce_y(lossless * half_ez + lossy * ez[...], -slope_ey)
    y_copies = send_y(1, left, right)
    z_charge, left, right = reduce_z(lossless * half_ex + lossy * ex[...], -slope_ez)
    z_copies = send_z(1, left, right)
    body = lossless * half_ey + lossy * ey[...]
    mean_ey = chain_solve(loader(x_fac), x_inverse, body - down_x(slope_ex), 2)
    next_ey = 2.0 * mean_ey - ey[...]
    y_returns, z_returns = half_lines(1, y_copies, z_copies)
    o_ey[...] = next_ey
    o_hz[...] = STEP * (flux_of_z + 2.0 * slope_ex - up_x(next_ey))

    arrive(y_returns)
    mean_ez, beyond_ez = expand_y(1, y_charge)
    next_ez = 2.0 * mean_ez - ez[...]
    o_ez[...] = next_ez
    above = 2.0 * beyond_ez - halo_y[0:1]
    o_hx[...] = STEP * (flux_of_x + 2.0 * slope_ey - up_y(next_ez, above))
    arrive(z_returns)
    mean_ex, beyond_ex = expand_z(1, z_charge)
    next_ex = 2.0 * mean_ex - ex[...]
    o_ex[...] = next_ex
    above = 2.0 * beyond_ex - halo_z[0]
    o_hy[...] = STEP * (flux_of_y + 2.0 * slope_ez - up_z(next_ex, above))

    for target, _, copy in halos:
        pl.when(target)(copy.wait_send)
    for copy in sent:
        copy.wait_send()


def deliver(*refs):
    held, results, sems = refs[:6], refs[6:12], refs[12]
    copies = [
        pltpu.make_async_copy(held[i], results[i], sems.at[i]) for i in range(6)
    ]
    for copy in copies:
        copy.start()
    for copy in copies:
        copy.wait()


def fused(rows, cols, *fields):
    ny, nz, nx = fields[0].shape
    f32 = jnp.float32
    block = (ny, nz, nx)
    y_levels, z_levels = len(levels_of(8)), len(levels_of(8))
    scratch = [
        (rows, 3, nx), (cols, 3, nx), (rows, 3, nx), (cols, 3, nx),
        (2, rows, 2, nx), (2, cols, 2, nx), (2, rows, 2, nx), (2, cols, 2, nx),
        (2, rows, 2, nx), (2, cols, 2, nx), (2, rows, 2, nx), (2, cols, 2, nx),
        (2, ny, 1, nx), (2, nz, nx), (2, ny, 1, nx),
        block, block, block, block,
        (len(levels_of(nz)),) + block, (len(levels_of(nz)),) + block,
        (2 * len(levels_of(nx)),) + block, (2 * y_levels, 8, nx), (2 * z_levels, 8, nx),
    ]
    held = pl.pallas_call(
        functools.partial(kernel, rows, cols),
        out_shape=[pltpu.VMEM(block, f32)] * 6,
        in_specs=[pl.BlockSpec(memory_space=pl.ANY)] * 8,
        out_specs=[pl.BlockSpec(memory_space=pltpu.VMEM)] * 6,
        scratch_shapes=[pltpu.VMEM(shape, f32) for shape in scratch]
        + [
            pltpu.SemaphoreType.DMA((2, 4)),
            pltpu.SemaphoreType.DMA((5, rows - 1)),
            pltpu.SemaphoreType.DMA((5, rows - 1)),
            pltpu.SemaphoreType.DMA((5, cols - 1)),
            pltpu.SemaphoreType.DMA((5, cols - 1)),
            pltpu.VMEM((8,) + block, f32),
            pltpu.SemaphoreType.DMA((8,)),
        ],
        compiler_params=pltpu.CompilerParams(
            collective_id=0, has_side_effects=True, vmem_limit_bytes=VMEM_LIMIT
        ),
        name="step",
    )(*[pltpu.with_memory_space_constraint(field, pltpu.HBM) for field in fields])
    return pl.pallas_call(
        deliver,
        out_shape=[jax.ShapeDtypeStruct(block, f32)] * 6,
        in_specs=[pl.BlockSpec(memory_space=pltpu.VMEM)] * 6,
        out_specs=[pl.BlockSpec(memory_space=pl.ANY)] * 6,
        scratch_shapes=[pltpu.SemaphoreType.DMA((6,))],
        compiler_params=pltpu.CompilerParams(vmem_limit_bytes=1024 * 1024),
        name="deliver",
    )(*held)


HALF_STEP = 30.0


def with_halo(cells, sides, width):
    for axis, dim in sides:
        count = lax.axis_size(axis)
        ends = count - 1
        head = lax.slice_in_dim(cells, 0, width, axis=dim)
        tail = lax.slice_in_dim(cells, cells.shape[dim] - width, cells.shape[dim], axis=dim)
        cells = jnp.concatenate(
            [
                lax.ppermute(tail, axis, [(i, (i + 1) % count) for i in range(ends)]),
                cells,
                lax.ppermute(head, axis, [((i + 1) % count, i) for i in range(ends)]),
            ],
            axis=dim,
        )
    return cells


def shifted(values, stride, line_axis, filler, forward):
    length = values.shape[line_axis]
    padding = jnp.full_like(lax.slice_in_dim(values, 0, stride, axis=line_axis), filler)
    if forward:
        return jnp.concatenate(
            [lax.slice_in_dim(values, stride, length, axis=line_axis), padding], line_axis
        )
    return jnp.concatenate(
        [padding, lax.slice_in_dim(values, 0, length - stride, axis=line_axis)], line_axis
    )


def diff_up(values, line_axis):
    return shifted(values, 1, line_axis, 0.0, True) - values


def diff_down(values, line_axis):
    return values - shifted(values, 1, line_axis, 0.0, False)


def reduce_lines(sub_diag, main_diag, super_diag, source, line_axis):
    length = source.shape[line_axis]
    stride = 1
    while stride < length:
        sub_lo = shifted(sub_diag, stride, line_axis, 0.0, False)
        mid_lo = shifted(main_diag, stride, line_axis, 1.0, False)
        sup_lo = shifted(super_diag, stride, line_axis, 0.0, False)
        src_lo = shifted(source, stride, line_axis, 0.0, False)
        sub_hi = shifted(sub_diag, stride, line_axis, 0.0, True)
        mid_hi = shifted(main_diag, stride, line_axis, 1.0, True)
        sup_hi = shifted(super_diag, stride, line_axis, 0.0, True)
        src_hi = shifted(source, stride, line_axis, 0.0, True)
        ratio_lo = sub_diag / mid_lo
        ratio_hi = super_diag / mid_hi
        sub_diag = -sub_lo * ratio_lo
        super_diag = -sup_hi * ratio_hi
        main_diag = main_diag - sup_lo * ratio_lo - sub_hi * ratio_hi
        source = source - src_lo * ratio_lo - src_hi * ratio_hi
        stride = stride * 2
    return source / main_diag


def line_flags(length, line_axis, rank):
    iota_shape = [1] * rank
    iota_shape[line_axis] = length
    where_line = lax.broadcasted_iota(jnp.int32, tuple(iota_shape), line_axis)
    return (where_line == 0, where_line == length - 1)


def line_system(coupling, is_first, is_final):
    sub_diag = jnp.where(is_first, 0.0, -coupling)
    main_diag = jnp.where(is_first, 1.0 + coupling, 1.0 + 2.0 * coupling)
    super_diag = jnp.where(is_final, 0.0, -coupling)
    return (sub_diag, main_diag, super_diag)


def solve_local(source, coupling, line_axis):
    is_first, is_final = line_flags(source.shape[line_axis], line_axis, source.ndim)
    sub_diag, main_diag, super_diag = line_system(coupling, is_first, is_final)
    return reduce_lines(sub_diag, main_diag, super_diag, source, line_axis)


def inner(values):
    return values[1:-1, 1:-1]


def with_faces(stacked):
    return with_halo(stacked, (("row", 1), ("col", 2)), 1)


def inside_mask(count_y, count_z):
    pos_y = (
        lax.axis_index("row") * count_y
        + lax.broadcasted_iota(jnp.int32, (count_y + 2, 1, 1), 0)
        - 1
    )
    pos_z = (
        lax.axis_index("col") * count_z
        + lax.broadcasted_iota(jnp.int32, (1, count_z + 2, 1), 1)
        - 1
    )
    inside = (
        (pos_y >= 0)
        & (pos_y < count_y * lax.axis_size("row"))
        & (pos_z >= 0)
        & (pos_z < count_z * lax.axis_size("col"))
    )
    return inside.astype(jnp.float32)


def solve_rows_moved(source, coupling):

    def along_lines(pieces):
        moved_source, moved_coupling = pieces
        turned_source = jnp.transpose(moved_source, (1, 2, 0))
        turned_coupling = jnp.transpose(moved_coupling, (1, 2, 0))
        solved = solve_local(turned_source, turned_coupling, 2)
        solved = jnp.transpose(solved, (2, 0, 1))
        return lax.all_to_all(solved, "row", split_axis=0, concat_axis=2, tiled=True)

    return along_lines(
        (
            lax.all_to_all(source, "row", split_axis=2, concat_axis=0, tiled=True),
            lax.all_to_all(coupling, "row", split_axis=2, concat_axis=0, tiled=True),
        )
    )


def solve_rows(source, coupling):
    return solve_rows_moved(source, coupling)


def solve_columns(source, coupling):

    def along_lines(pieces):
        moved_source, moved_coupling = pieces
        solved = solve_local(moved_source, moved_coupling, 1)
        return lax.all_to_all(solved, "col", split_axis=1, concat_axis=2, tiled=True)

    return along_lines(
        (
            lax.all_to_all(source, "col", split_axis=2, concat_axis=1, tiled=True),
            lax.all_to_all(coupling, "col", split_axis=2, concat_axis=1, tiled=True),
        )
    )


def on_device(
    efield_x, efield_y, efield_z, hfield_x, hfield_y, hfield_z, permittivity, conductivity
):
    count_y = efield_x.shape[0]
    count_z = efield_x.shape[1]
    damping = conductivity * HALF_STEP / (2.0 * permittivity)
    keep_coef = (1.0 - damping) / (1.0 + damping)
    drive_coef = HALF_STEP / (permittivity * (1.0 + damping))
    coupling = drive_coef * HALF_STEP
    old_all = with_faces(jnp.stack([efield_x, efield_y, efield_z, hfield_x, hfield_y, hfield_z]))
    old_ex, old_ey, old_ez = (old_all[0], old_all[1], old_all[2])
    old_hx, old_hy, old_hz = (old_all[3], old_all[4], old_all[5])
    source_x = keep_coef * efield_x + drive_coef * (
        inner(diff_down(old_hz, 0))
        - inner(diff_down(old_hy, 1))
        - HALF_STEP * inner(diff_down(diff_up(old_ey, 2), 0))
    )
    source_y = keep_coef * efield_y + drive_coef * (
        inner(diff_down(old_hx, 1))
        - diff_down(hfield_z, 2)
        - HALF_STEP * inner(diff_down(diff_up(old_ez, 0), 1))
    )
    source_z = keep_coef * efield_z + drive_coef * (
        diff_down(hfield_y, 2)
        - inner(diff_down(old_hx, 0))
        - HALF_STEP * inner(diff_down(diff_up(old_ex, 1), 2))
    )
    half_ex = solve_rows(source_x, coupling)
    half_ey = solve_columns(source_y, coupling)
    half_ez = solve_local(source_z, coupling, 2)
    mid_all = with_faces(jnp.stack([half_ex, half_ey, half_ez]))
    mid_ex, mid_ey, mid_ez = (mid_all[0], mid_all[1], mid_all[2])
    inside = inside_mask(count_y, count_z)
    dz_mid_ey = diff_up(mid_ey, 1)
    dx_mid_ez = diff_up(mid_ez, 2)
    dy_mid_ex = diff_up(mid_ex, 0)
    mid_hx = (old_hx + HALF_STEP * (dz_mid_ey - diff_up(old_ez, 0))) * inside
    mid_hy = (old_hy + HALF_STEP * (dx_mid_ez - diff_up(old_ex, 1))) * inside
    mid_hz = (old_hz + HALF_STEP * (dy_mid_ex - diff_up(old_ey, 2))) * inside
    second_x = keep_coef * half_ex + drive_coef * (
        inner(diff_down(mid_hz, 0))
        - inner(diff_down(mid_hy, 1))
        - HALF_STEP * inner(diff_down(dx_mid_ez, 1))
    )
    second_y = keep_coef * half_ey + drive_coef * (
        inner(diff_down(mid_hx, 1))
        - inner(diff_down(mid_hz, 2))
        - HALF_STEP * inner(diff_down(dy_mid_ex, 2))
    )
    second_z = keep_coef * half_ez + drive_coef * (
        inner(diff_down(mid_hy, 2))
        - inner(diff_down(mid_hx, 0))
        - HALF_STEP * inner(diff_down(dz_mid_ey, 0))
    )
    next_ex = solve_columns(second_x, coupling)
    next_ey = solve_local(second_y, coupling, 2)
    next_ez = solve_rows(second_z, coupling)
    last_all = with_faces(jnp.stack([next_ex, next_ez]))
    next_hx = inner(mid_hx) + HALF_STEP * (inner(dz_mid_ey) - inner(diff_up(last_all[1], 0)))
    next_hy = inner(mid_hy) + HALF_STEP * (inner(dx_mid_ez) - inner(diff_up(last_all[0], 1)))
    next_hz = inner(mid_hz) + HALF_STEP * (inner(dy_mid_ex) - diff_up(next_ey, 2))
    return (next_ex, next_ey, next_ez, next_hx, next_hy, next_hz)


def solution(mesh):
    rows, cols = mesh.shape["row"], mesh.shape["col"]
    placed = (
        P("row", "col", None),
        P("row", "col", None),
        P("row", "col", None),
        P("row", "col", None),
        P("row", "col", None),
        P("row", "col", None),
        P("row", "col", None),
        P("row", "col", None),
    )

    def per_device(*fields):
        ny, nz = fields[0].shape[:2]
        if nz == rows == 8 and ny == cols and 1 < cols < 8:
            return tuple(fused(rows, cols, *fields))
        return on_device(*fields)

    return jax.shard_map(
        per_device,
        mesh=mesh,
        in_specs=placed,
        out_specs=(
            P("row", "col", None),
            P("row", "col", None),
            P("row", "col", None),
            P("row", "col", None),
            P("row", "col", None),
            P("row", "col", None),
        ),
        check_vma=False,
    )
```

```python
import functools

import jax
import jax.numpy as jnp
from jax import lax
from jax.experimental import pallas as pl
from jax.experimental.pallas import tpu as pltpu
from jax.sharding import PartitionSpec as P

STEP = 30.0
MESH = pl.DeviceIdType.MESH
SIDE = 15.0
VMEM_LIMIT = 40 * 1024 * 1024
AREA = 900.0


def roll_to(values, stride, axis):
    return pltpu.roll(values, stride % values.shape[axis], axis)


def edge(shape, axis, where_at):
    return lax.broadcasted_iota(jnp.int32, shape, axis) == where_at


def up_x(values):
    last = edge(values.shape, 2, values.shape[2] - 1)
    return jnp.where(last, 0.0, roll_to(values, -1, 2)) - values


def down_x(values):
    return values - jnp.where(edge(values.shape, 2, 0), 0.0, roll_to(values, 1, 2))


def up_z(values, above):
    last = edge(values.shape, 1, values.shape[1] - 1)
    return jnp.where(last, above, roll_to(values, -1, 1)) - values


def down_z(values, below):
    return values - jnp.where(edge(values.shape, 1, 0), below, roll_to(values, 1, 1))


def up_y(values, above):
    return jnp.concatenate([values[1:], above], 0) - values


def down_y(values, below):
    return values - jnp.concatenate([below, values[:-1]], 0)


def levels_of(length):
    strides = []
    while (1 << len(strides)) < length:
        strides.append(1 << len(strides))
    return strides


def chain_factors(link, excess, axis, keep):
    for level, stride in enumerate(levels_of(link.shape[axis])):
        link_hi = roll_to(link, -stride, axis)
        inverse = 1.0 / (link + link_hi + excess)
        ratio_lo = link * roll_to(inverse, stride, axis)
        ratio_hi = roll_to(link * inverse, -stride, axis)
        keep(2 * level, ratio_lo)
        keep(2 * level + 1, ratio_hi)
        excess = (
            excess
            + ratio_lo * roll_to(excess, stride, axis)
            + ratio_hi * roll_to(excess, -stride, axis)
        )
        link = ratio_lo * roll_to(link, stride, axis)
    return 1.0 / excess


def chain_solve(load, inverse, load_source, axis):
    source = load_source
    for level, stride in enumerate(levels_of(source.shape[axis])):
        source = (
            source
            + load(2 * level) * roll_to(source, stride, axis)
            + load(2 * level + 1) * roll_to(source, -stride, axis)
        )
    return source * inverse


def kernel(
    rows, cols,
    *refs,
):
    hbm = refs[:8]
    (
    o_ex, o_ey, o_ez, o_hx, o_hy, o_hz,
    y_mat, z_mat, y_mat_in, z_mat_in,
    y_src, z_src, y_src_in, z_src_in,
    y_out, z_out, y_back,
    face_z, halo_y, halo_z,
    y_alpha, y_beta, z_alpha, z_beta, z_fwd, z_bwd,
    x_fac, y_fac, z_fac,
    halo_sems, row_send, row_recv, col_send, col_recv,
    fields, field_sems,
    ) = refs[8:]
    ex, ey, ez, hx, hy, hz, eps, sig = [fields.at[i] for i in range(8)]
    loads = [
        pltpu.make_async_copy(hbm[i], fields.at[i], field_sems.at[i]) for i in range(8)
    ]
    for i in (6, 7, 0, 4, 2, 3, 5, 1):
        loads[i].start()
    ny, nz, nx = ex.shape
    r = lax.axis_index("row")
    c = lax.axis_index("col")
    zero_y = jnp.zeros(halo_y.shape, jnp.float32)
    zero_z = jnp.zeros(halo_z.shape, jnp.float32)
    halo_y[...] = zero_y
    halo_z[...] = zero_z
    barrier = pltpu.get_barrier_semaphore()
    for d in range(1, rows):
        pl.semaphore_signal(
            barrier, inc=1, device_id=(lax.rem(r + d, rows), c), device_id_type=MESH
        )
    for d in range(1, cols):
        pl.semaphore_signal(
            barrier, inc=1, device_id=(r, lax.rem(c + d, cols)), device_id_type=MESH
        )

    def halo(number, source, target, device):
        return pltpu.make_async_remote_copy(
            src_ref=source, dst_ref=target,
            send_sem=halo_sems.at[0, number], recv_sem=halo_sems.at[1, number],
            device_id=device, device_id_type=MESH,
        )

    low_r, high_r = jnp.maximum(r - 1, 0), jnp.minimum(r + 1, rows - 1)
    low_c, high_c = jnp.maximum(c - 1, 0), jnp.minimum(c + 1, cols - 1)
    halos = [
        (r > 0, r < rows - 1, halo(0, ez.at[0], halo_y.at[0], (low_r, c))),
        (c < cols - 1, c > 0, halo(1, face_z.at[1], halo_z.at[1], (r, high_c))),
        (r < rows - 1, r > 0, halo(2, hx.at[ny - 1], halo_y.at[1], (high_r, c))),
        (c > 0, c < cols - 1, halo(3, face_z.at[0], halo_z.at[0], (r, low_c))),
    ]

    def start_halos():
        for target, _, copy in halos:
            pl.when(target)(copy.start)

    def wait_halo(number):
        target, sender, copy = halos[number]
        pl.when(sender)(copy.wait_recv)

    sent = []

    def exchange(step, axis, source, target):
        if axis == "row":
            count, me, send, recv = rows, r, row_send, row_recv
        else:
            count, me, send, recv = cols, c, col_send, col_recv
        copies = []
        for d in range(1, count):
            peer = lax.rem(me + d, count)
            copies.append(
                pltpu.make_async_remote_copy(
                    src_ref=source.at[peer] if axis == "row" else source,
                    dst_ref=target.at[me],
                    send_sem=send.at[step, d - 1], recv_sem=recv.at[step, d - 1],
                    device_id=(peer, c) if axis == "row" else (r, peer),
                    device_id_type=MESH,
                )
            )
        for copy in copies:
            copy.start()
        target[me] = source[me] if axis == "row" else source[...]
        sent.extend(copies)
        return copies

    def arrive(copies):
        for copy in copies:
            copy.wait_recv()

    loads[6].wait()
    loads[7].wait()
    ground = (eps[...] + SIDE * sig[...]) * (1.0 / AREA)
    link = jnp.ones((nz, nx), jnp.float32)
    left = ground[0]
    carry = ground[1] * 0.0
    for j in range(1, ny):
        here = ground[j] + carry
        beta = 1.0 / (link + 1.0 + here)
        alpha = link * beta
        y_alpha[j] = alpha
        y_beta[j] = beta
        left = left + alpha * here
        carry = beta * here
        link = alpha
    for p in range(rows):
        y_mat[p, 0:1, :] = link[p : p + 1]
        y_mat[p, 1:2, :] = left[p : p + 1]
        y_mat[p, 2:3, :] = carry[p : p + 1]
    for i in (0, 4, 2, 3):
        loads[i].wait()
    face_z[0] = ex[:, 0:1, :]
    face_z[1] = hy[:, nz - 1 : nz, :]
    pl.semaphore_wait(barrier, rows - 1 + cols - 1)
    start_halos()
    y_mat_copies = exchange(0, "row", y_mat, y_mat_in)

    spot = lax.broadcasted_iota(jnp.int32, (ny, nz, nx), 1)
    here = ground
    link = jnp.ones((ny, nz, nx), jnp.float32)
    beta = jnp.ones((ny, nz, nx), jnp.float32)
    for j in range(1, nz):
        flow = beta * here if j > 1 else jnp.zeros_like(here)
        fresh_link = link if j == 1 else roll_to(link * beta, 1, 1)
        fresh = ground + roll_to(flow, 1, 1)
        here = jnp.where(spot == j, fresh, here)
        link = jnp.where(spot == j, fresh_link, link)
        beta = jnp.where(spot == j, 1.0 / (link + 1.0 + here), beta)
    first = spot == 0
    beta = jnp.where(first, 0.0, beta)
    alpha = link * beta
    z_alpha[...] = alpha
    z_beta[...] = beta
    left = jnp.sum(jnp.where(first, ground, alpha * here), axis=1)
    tail = beta * here
    z_mat[0] = alpha[:, nz - 1, :]
    z_mat[1] = left
    z_mat[2] = tail[:, nz - 1, :]
    z_mat_copies = exchange(0, "col", z_mat, z_mat_in)
    forward = jnp.where(first, 0.0, roll_to(beta, 1, 1))
    backward = jnp.where(spot == nz - 1, 0.0, beta)
    for level, stride in enumerate(levels_of(nz)):
        z_fwd[level] = forward
        z_bwd[level] = backward
        forward = forward * jnp.where(spot < stride, 0.0, roll_to(forward, stride, 1))
        backward = backward * jnp.where(
            spot >= nz - stride, 0.0, roll_to(backward, -stride, 1)
        )

    def reduce_y(body, flux):
        charge = []
        left = body[0] + flux[0]
        for j in range(1, ny):
            now = body[j] + flux[j] - flux[j - 1]
            if j > 1:
                now = now + y_beta[j - 1] * charge[-1]
            charge.append(now)
            left = left + y_alpha[j] * now
        right = y_beta[ny - 1] * charge[-1] - flux[ny - 1]
        return charge, left, right

    def send_y(stage, left, right):
        for p in range(rows):
            y_src[stage, p, 0:1, :] = left[p : p + 1]
            y_src[stage, p, 1:2, :] = right[p : p + 1]
        return exchange(1 + 2 * stage, "row", y_src.at[stage], y_src_in.at[stage])

    def expand_y(stage, charge):
        near = jnp.concatenate([y_back[stage, p, 0:1, :] for p in range(rows)], 0)
        beyond = jnp.concatenate([y_back[stage, p, 1:2, :] for p in range(rows)], 0)
        cells = []
        after = beyond
        for j in range(ny - 1, 0, -1):
            after = y_alpha[j] * near + y_beta[j] * (after + charge[j - 1])
            cells.insert(0, after)
        return jnp.stack([near] + cells, 0), beyond[None]

    def reduce_z(body, flux):
        source = body + flux - jnp.where(first, 0.0, roll_to(flux, 1, 1))
        charge = jnp.where(first, 0.0, source)
        for level, stride in enumerate(levels_of(nz)):
            charge = charge + z_fwd[level] * roll_to(charge, stride, 1)
        left = jnp.sum(jnp.where(first, source, z_alpha[...] * charge), axis=1)
        right = z_beta[...] * charge - flux
        return charge, left, right

    def send_z(stage, left, right):
        z_src[stage, 0] = left
        z_src[stage, 1] = right[:, nz - 1, :]
        return exchange(1 + 2 * stage, "col", z_src.at[stage], z_src_in.at[stage])

    def expand_z(stage, charge):
        near = z_out[stage, c][:, None, :]
        beyond = z_out[stage, c + 1][:, None, :]
        cells = z_alpha[...] * near + z_beta[...] * charge
        cells = cells + jnp.where(spot == nz - 1, z_beta[...] * beyond, 0.0)
        cells = jnp.where(first, near, cells)
        for level, stride in enumerate(levels_of(nz)):
            cells = cells + z_bwd[level] * roll_to(cells, -stride, 1)
        return cells, beyond

    tall = 8

    def rows_of(buffer, number, count, filler):
        parts = [buffer[p, number : number + 1, :] for p in range(count)]
        if count < tall:
            parts.append(jnp.full((tall - count, nx), filler, jnp.float32))
        return jnp.concatenate(parts, 0)

    def line_factors(buffer, count, keep):
        row = lax.broadcasted_iota(jnp.int32, (tall, nx), 0)
        link = rows_of(buffer, 0, count, 0.0)
        left = rows_of(buffer, 1, count, 1.0)
        right = rows_of(buffer, 2, count, 0.0)
        below = row == 0
        excess = left + jnp.where(below, 0.0, roll_to(right, 1, 0))
        excess = excess + jnp.where(row == count - 1, link, 0.0)
        inner_link = jnp.where(below | (row >= count), 0.0, roll_to(link, 1, 0))
        return chain_factors(inner_link, excess, 0, keep)

    def line_solve(stage, source_in, count, load, inverse, out):
        row = lax.broadcasted_iota(jnp.int32, (tall, nx), 0)
        left = rows_of(source_in.at[stage], 0, count, 0.0)
        right = rows_of(source_in.at[stage], 1, count, 0.0)
        source = left + jnp.where(row == 0, 0.0, roll_to(right, 1, 0))
        source = jnp.where(row < count, source, 0.0)
        near = chain_solve(load, inverse, source, 0)
        for p in range(count):
            out[stage, p, 0:1, :] = near[p : p + 1]
            if p < count - 1:
                out[stage, p, 1:2, :] = near[p + 1 : p + 2]
            else:
                out[stage, p, 1:2, :] = jnp.zeros((1, nx), jnp.float32)

    def keeper(ref):
        def keep(number, values):
            ref[number] = values
        return keep

    def loader(ref):
        def load(number):
            return ref[number]
        return load

    first_x = lax.broadcasted_iota(jnp.int32, (ny, nz, nx), 2) == 0
    last_x = lax.broadcasted_iota(jnp.int32, (ny, nz, nx), 2) == nx - 1
    x_inverse = chain_factors(
        jnp.where(first_x, 0.0, 1.0), ground + jnp.where(last_x, 1.0, 0.0), 2, keeper(x_fac)
    )

    loads[5].wait()
    loads[1].wait()
    keep_ground = (eps[...] - SIDE * sig[...]) * (1.0 / AREA)
    flux_of_z = hz[...] * (1.0 / STEP) - up_x(ey[...])
    wait_halo(1)
    body = keep_ground * ex[...] - down_z(hy[...], halo_z[1]) * (1.0 / STEP)
    y_charge, left, right = reduce_y(body, flux_of_z)
    y_copies = send_y(0, left, right)
    wait_halo(0)
    flux_of_x = hx[...] * (1.0 / STEP) - up_y(ez[...], halo_y[0:1])
    body = keep_ground * ey[...] - down_x(hz[...]) * (1.0 / STEP)
    z_charge, left, right = reduce_z(body, flux_of_x)
    z_copies = send_z(0, left, right)

    wait_halo(2)
    wait_halo(3)
    flux_of_y = hy[...] * (1.0 / STEP) - up_z(ex[...], halo_z[0])
    body = keep_ground * ez[...] - down_y(hx[...], halo_y[1:2]) * (1.0 / STEP)
    half_ez = chain_solve(loader(x_fac), x_inverse, body + down_x(flux_of_y), 2)
    slope_ez = up_x(half_ez)

    arrive(y_mat_copies)
    y_inverse = line_factors(y_mat_in, rows, keeper(y_fac))
    arrive(z_mat_copies)
    grounded = z_mat_in[0, 1]
    for q in range(cols):
        link = z_mat_in[q, 0]
        inverse = 1.0 / (grounded + link)
        z_fac[0, q] = link * inverse
        z_fac[1, q] = inverse
        if q < cols - 1:
            grounded = z_mat_in[q + 1, 1] + z_mat_in[q, 2] + link * inverse * grounded

    def half_lines(stage, y_copies, z_copies):
        arrive(y_copies)
        line_solve(stage, y_src_in, rows, loader(y_fac), y_inverse, y_out)
        y_returns = exchange(2 + 2 * stage, "row", y_out.at[stage], y_back.at[stage])
        arrive(z_copies)
        source = [z_src_in[stage, 0, 0]]
        for q in range(1, cols):
            own = z_src_in[stage, q, 0] + z_src_in[stage, q - 1, 1]
            source.append(own + z_fac[0, q - 1] * source[-1])
        value = jnp.zeros((ny, nx), jnp.float32)
        z_out[stage, cols] = value
        for q in range(cols - 1, -1, -1):
            value = z_fac[1, q] * source[q] + z_fac[0, q] * value
            z_out[stage, q] = value
        return y_returns

    y_returns = half_lines(0, y_copies, z_copies)

    arrive(y_returns)
    half_ex, beyond_ex = expand_y(0, y_charge)
    slope_ex = up_y(half_ex, beyond_ex)
    half_ey, beyond_ey = expand_z(0, z_charge)
    slope_ey = up_z(half_ey, beyond_ey)

    lossless = eps[...] * (1.0 / AREA)
    lossy = sig[...] * (SIDE / AREA)
    y_charge, left, right = reduce_y(lossless * half_ez + lossy * ez[...], -slope_ey)
    y_copies = send_y(1, left, right)
    z_charge, left, right = reduce_z(lossless * half_ex + lossy * ex[...], -slope_ez)
    z_copies = send_z(1, left, right)
    body = lossless * half_ey + lossy * ey[...]
    mean_ey = chain_solve(loader(x_fac), x_inverse, body - down_x(slope_ex), 2)
    next_ey = 2.0 * mean_ey - ey[...]
    y_returns = half_lines(1, y_copies, z_copies)
    o_ey[...] = next_ey
    o_hz[...] = STEP * (flux_of_z + 2.0 * slope_ex - up_x(next_ey))

    arrive(y_returns)
    mean_ez, beyond_ez = expand_y(1, y_charge)
    next_ez = 2.0 * mean_ez - ez[...]
    o_ez[...] = next_ez
    above = 2.0 * beyond_ez - halo_y[0:1]
    o_hx[...] = STEP * (flux_of_x + 2.0 * slope_ey - up_y(next_ez, above))
    mean_ex, beyond_ex = expand_z(1, z_charge)
    next_ex = 2.0 * mean_ex - ex[...]
    o_ex[...] = next_ex
    above = 2.0 * beyond_ex - halo_z[0]
    o_hy[...] = STEP * (flux_of_y + 2.0 * slope_ez - up_z(next_ex, above))

    for target, _, copy in halos:
        pl.when(target)(copy.wait_send)
    for copy in sent:
        copy.wait_send()


def deliver(*refs):
    held, results, sems = refs[:6], refs[6:12], refs[12]
    copies = [
        pltpu.make_async_copy(held[i], results[i], sems.at[i]) for i in range(6)
    ]
    for copy in copies:
        copy.start()
    for copy in copies:
        copy.wait()


def fused(rows, cols, *fields):
    ny, nz, nx = fields[0].shape
    f32 = jnp.float32
    block = (ny, nz, nx)
    y_levels = len(levels_of(8))
    scratch = [
        (rows, 3, nx), (3, ny, nx), (rows, 3, nx), (cols, 3, ny, nx),
        (2, rows, 2, nx), (2, 2, ny, nx), (2, rows, 2, nx), (2, cols, 2, ny, nx),
        (2, rows, 2, nx), (2, cols + 1, ny, nx), (2, rows, 2, nx),
        (2, ny, 1, nx), (2, nz, nx), (2, ny, 1, nx),
        block, block, block, block,
        (len(levels_of(nz)),) + block, (len(levels_of(nz)),) + block,
        (2 * len(levels_of(nx)),) + block, (2 * y_levels, 8, nx), (2, cols, ny, nx),
    ]
    held = pl.pallas_call(
        functools.partial(kernel, rows, cols),
        out_shape=[pltpu.VMEM(block, f32)] * 6,
        in_specs=[pl.BlockSpec(memory_space=pl.ANY)] * 8,
        out_specs=[pl.BlockSpec(memory_space=pltpu.VMEM)] * 6,
        scratch_shapes=[pltpu.VMEM(shape, f32) for shape in scratch]
        + [
            pltpu.SemaphoreType.DMA((2, 4)),
            pltpu.SemaphoreType.DMA((5, rows - 1)),
            pltpu.SemaphoreType.DMA((5, rows - 1)),
            pltpu.SemaphoreType.DMA((5, cols - 1)),
            pltpu.SemaphoreType.DMA((5, cols - 1)),
            pltpu.VMEM((8,) + block, f32),
            pltpu.SemaphoreType.DMA((8,)),
        ],
        compiler_params=pltpu.CompilerParams(
            collective_id=0, has_side_effects=True, vmem_limit_bytes=VMEM_LIMIT
        ),
        name="step",
    )(*[pltpu.with_memory_space_constraint(field, pltpu.HBM) for field in fields])
    return pl.pallas_call(
        deliver,
        out_shape=[jax.ShapeDtypeStruct(block, f32)] * 6,
        in_specs=[pl.BlockSpec(memory_space=pltpu.VMEM)] * 6,
        out_specs=[pl.BlockSpec(memory_space=pl.ANY)] * 6,
        scratch_shapes=[pltpu.SemaphoreType.DMA((6,))],
        compiler_params=pltpu.CompilerParams(vmem_limit_bytes=1024 * 1024),
        name="deliver",
    )(*held)


HALF_STEP = 30.0


def with_halo(cells, sides, width):
    for axis, dim in sides:
        count = lax.axis_size(axis)
        ends = count - 1
        head = lax.slice_in_dim(cells, 0, width, axis=dim)
        tail = lax.slice_in_dim(cells, cells.shape[dim] - width, cells.shape[dim], axis=dim)
        cells = jnp.concatenate(
            [
                lax.ppermute(tail, axis, [(i, (i + 1) % count) for i in range(ends)]),
                cells,
                lax.ppermute(head, axis, [((i + 1) % count, i) for i in range(ends)]),
            ],
            axis=dim,
        )
    return cells


def shifted(values, stride, line_axis, filler, forward):
    length = values.shape[line_axis]
    padding = jnp.full_like(lax.slice_in_dim(values, 0, stride, axis=line_axis), filler)
    if forward:
        return jnp.concatenate(
            [lax.slice_in_dim(values, stride, length, axis=line_axis), padding], line_axis
        )
    return jnp.concatenate(
        [padding, lax.slice_in_dim(values, 0, length - stride, axis=line_axis)], line_axis
    )


def diff_up(values, line_axis):
    return shifted(values, 1, line_axis, 0.0, True) - values


def diff_down(values, line_axis):
    return values - shifted(values, 1, line_axis, 0.0, False)


def reduce_lines(sub_diag, main_diag, super_diag, source, line_axis):
    length = source.shape[line_axis]
    stride = 1
    while stride < length:
        sub_lo = shifted(sub_diag, stride, line_axis, 0.0, False)
        mid_lo = shifted(main_diag, stride, line_axis, 1.0, False)
        sup_lo = shifted(super_diag, stride, line_axis, 0.0, False)
        src_lo = shifted(source, stride, line_axis, 0.0, False)
        sub_hi = shifted(sub_diag, stride, line_axis, 0.0, True)
        mid_hi = shifted(main_diag, stride, line_axis, 1.0, True)
        sup_hi = shifted(super_diag, stride, line_axis, 0.0, True)
        src_hi = shifted(source, stride, line_axis, 0.0, True)
        ratio_lo = sub_diag / mid_lo
        ratio_hi = super_diag / mid_hi
        sub_diag = -sub_lo * ratio_lo
        super_diag = -sup_hi * ratio_hi
        main_diag = main_diag - sup_lo * ratio_lo - sub_hi * ratio_hi
        source = source - src_lo * ratio_lo - src_hi * ratio_hi
        stride = stride * 2
    return source / main_diag


def line_flags(length, line_axis, rank):
    iota_shape = [1] * rank
    iota_shape[line_axis] = length
    where_line = lax.broadcasted_iota(jnp.int32, tuple(iota_shape), line_axis)
    return (where_line == 0, where_line == length - 1)


def line_system(coupling, is_first, is_final):
    sub_diag = jnp.where(is_first, 0.0, -coupling)
    main_diag = jnp.where(is_first, 1.0 + coupling, 1.0 + 2.0 * coupling)
    super_diag = jnp.where(is_final, 0.0, -coupling)
    return (sub_diag, main_diag, super_diag)


def solve_local(source, coupling, line_axis):
    is_first, is_final = line_flags(source.shape[line_axis], line_axis, source.ndim)
    sub_diag, main_diag, super_diag = line_system(coupling, is_first, is_final)
    return reduce_lines(sub_diag, main_diag, super_diag, source, line_axis)


def inner(values):
    return values[1:-1, 1:-1]


def with_faces(stacked):
    return with_halo(stacked, (("row", 1), ("col", 2)), 1)


def inside_mask(count_y, count_z):
    pos_y = (
        lax.axis_index("row") * count_y
        + lax.broadcasted_iota(jnp.int32, (count_y + 2, 1, 1), 0)
        - 1
    )
    pos_z = (
        lax.axis_index("col") * count_z
        + lax.broadcasted_iota(jnp.int32, (1, count_z + 2, 1), 1)
        - 1
    )
    inside = (
        (pos_y >= 0)
        & (pos_y < count_y * lax.axis_size("row"))
        & (pos_z >= 0)
        & (pos_z < count_z * lax.axis_size("col"))
    )
    return inside.astype(jnp.float32)


def solve_rows_moved(source, coupling):

    def along_lines(pieces):
        moved_source, moved_coupling = pieces
        turned_source = jnp.transpose(moved_source, (1, 2, 0))
        turned_coupling = jnp.transpose(moved_coupling, (1, 2, 0))
        solved = solve_local(turned_source, turned_coupling, 2)
        solved = jnp.transpose(solved, (2, 0, 1))
        return lax.all_to_all(solved, "row", split_axis=0, concat_axis=2, tiled=True)

    return along_lines(
        (
            lax.all_to_all(source, "row", split_axis=2, concat_axis=0, tiled=True),
            lax.all_to_all(coupling, "row", split_axis=2, concat_axis=0, tiled=True),
        )
    )


def solve_rows(source, coupling):
    return solve_rows_moved(source, coupling)


def solve_columns(source, coupling):

    def along_lines(pieces):
        moved_source, moved_coupling = pieces
        solved = solve_local(moved_source, moved_coupling, 1)
        return lax.all_to_all(solved, "col", split_axis=1, concat_axis=2, tiled=True)

    return along_lines(
        (
            lax.all_to_all(source, "col", split_axis=2, concat_axis=1, tiled=True),
            lax.all_to_all(coupling, "col", split_axis=2, concat_axis=1, tiled=True),
        )
    )


def on_device(
    efield_x, efield_y, efield_z, hfield_x, hfield_y, hfield_z, permittivity, conductivity
):
    count_y = efield_x.shape[0]
    count_z = efield_x.shape[1]
    damping = conductivity * HALF_STEP / (2.0 * permittivity)
    keep_coef = (1.0 - damping) / (1.0 + damping)
    drive_coef = HALF_STEP / (permittivity * (1.0 + damping))
    coupling = drive_coef * HALF_STEP
    old_all = with_faces(jnp.stack([efield_x, efield_y, efield_z, hfield_x, hfield_y, hfield_z]))
    old_ex, old_ey, old_ez = (old_all[0], old_all[1], old_all[2])
    old_hx, old_hy, old_hz = (old_all[3], old_all[4], old_all[5])
    source_x = keep_coef * efield_x + drive_coef * (
        inner(diff_down(old_hz, 0))
        - inner(diff_down(old_hy, 1))
        - HALF_STEP * inner(diff_down(diff_up(old_ey, 2), 0))
    )
    source_y = keep_coef * efield_y + drive_coef * (
        inner(diff_down(old_hx, 1))
        - diff_down(hfield_z, 2)
        - HALF_STEP * inner(diff_down(diff_up(old_ez, 0), 1))
    )
    source_z = keep_coef * efield_z + drive_coef * (
        diff_down(hfield_y, 2)
        - inner(diff_down(old_hx, 0))
        - HALF_STEP * inner(diff_down(diff_up(old_ex, 1), 2))
    )
    half_ex = solve_rows(source_x, coupling)
    half_ey = solve_columns(source_y, coupling)
    half_ez = solve_local(source_z, coupling, 2)
    mid_all = with_faces(jnp.stack([half_ex, half_ey, half_ez]))
    mid_ex, mid_ey, mid_ez = (mid_all[0], mid_all[1], mid_all[2])
    inside = inside_mask(count_y, count_z)
    dz_mid_ey = diff_up(mid_ey, 1)
    dx_mid_ez = diff_up(mid_ez, 2)
    dy_mid_ex = diff_up(mid_ex, 0)
    mid_hx = (old_hx + HALF_STEP * (dz_mid_ey - diff_up(old_ez, 0))) * inside
    mid_hy = (old_hy + HALF_STEP * (dx_mid_ez - diff_up(old_ex, 1))) * inside
    mid_hz = (old_hz + HALF_STEP * (dy_mid_ex - diff_up(old_ey, 2))) * inside
    second_x = keep_coef * half_ex + drive_coef * (
        inner(diff_down(mid_hz, 0))
        - inner(diff_down(mid_hy, 1))
        - HALF_STEP * inner(diff_down(dx_mid_ez, 1))
    )
    second_y = keep_coef * half_ey + drive_coef * (
        inner(diff_down(mid_hx, 1))
        - inner(diff_down(mid_hz, 2))
        - HALF_STEP * inner(diff_down(dy_mid_ex, 2))
    )
    second_z = keep_coef * half_ez + drive_coef * (
        inner(diff_down(mid_hy, 2))
        - inner(diff_down(mid_hx, 0))
        - HALF_STEP * inner(diff_down(dz_mid_ey, 0))
    )
    next_ex = solve_columns(second_x, coupling)
    next_ey = solve_local(second_y, coupling, 2)
    next_ez = solve_rows(second_z, coupling)
    last_all = with_faces(jnp.stack([next_ex, next_ez]))
    next_hx = inner(mid_hx) + HALF_STEP * (inner(dz_mid_ey) - inner(diff_up(last_all[1], 0)))
    next_hy = inner(mid_hy) + HALF_STEP * (inner(dx_mid_ez) - inner(diff_up(last_all[0], 1)))
    next_hz = inner(mid_hz) + HALF_STEP * (inner(dy_mid_ex) - diff_up(next_ey, 2))
    return (next_ex, next_ey, next_ez, next_hx, next_hy, next_hz)


def solution(mesh):
    rows, cols = mesh.shape["row"], mesh.shape["col"]
    placed = (
        P("row", "col", None),
        P("row", "col", None),
        P("row", "col", None),
        P("row", "col", None),
        P("row", "col", None),
        P("row", "col", None),
        P("row", "col", None),
        P("row", "col", None),
    )

    def per_device(*fields):
        ny, nz = fields[0].shape[:2]
        if nz == rows == 8 and ny == cols and 1 < cols < 8:
            return tuple(fused(rows, cols, *fields))
        return on_device(*fields)

    return jax.shard_map(
        per_device,
        mesh=mesh,
        in_specs=placed,
        out_specs=(
            P("row", "col", None),
            P("row", "col", None),
            P("row", "col", None),
            P("row", "col", None),
            P("row", "col", None),
            P("row", "col", None),
        ),
        check_vma=False,
    )
```

```python
import functools

import jax
import jax.numpy as jnp
from jax import lax
from jax.experimental import pallas as pl
from jax.experimental.pallas import tpu as pltpu
from jax.sharding import PartitionSpec as P

STEP = 30.0
MESH = pl.DeviceIdType.MESH
SIDE = 15.0
VMEM_LIMIT = 40 * 1024 * 1024
AREA = 900.0


def roll_to(values, stride, axis):
    return pltpu.roll(values, stride % values.shape[axis], axis)


def edge(shape, axis, where_at):
    return lax.broadcasted_iota(jnp.int32, shape, axis) == where_at


def up_x(values):
    last = edge(values.shape, 2, values.shape[2] - 1)
    return jnp.where(last, 0.0, roll_to(values, -1, 2)) - values


def down_x(values):
    return values - jnp.where(edge(values.shape, 2, 0), 0.0, roll_to(values, 1, 2))


def up_z(values, above):
    last = edge(values.shape, 1, values.shape[1] - 1)
    return jnp.where(last, above, roll_to(values, -1, 1)) - values


def down_z(values, below):
    return values - jnp.where(edge(values.shape, 1, 0), below, roll_to(values, 1, 1))


def up_y(values, above):
    return jnp.concatenate([values[1:], above], 0) - values


def down_y(values, below):
    return values - jnp.concatenate([below, values[:-1]], 0)


def levels_of(length):
    strides = []
    while (1 << len(strides)) < length:
        strides.append(1 << len(strides))
    return strides


def chain_factors(link, excess, axis, keep):
    for level, stride in enumerate(levels_of(link.shape[axis])):
        link_hi = roll_to(link, -stride, axis)
        inverse = 1.0 / (link + link_hi + excess)
        ratio_lo = link * roll_to(inverse, stride, axis)
        ratio_hi = roll_to(link * inverse, -stride, axis)
        keep(2 * level, ratio_lo)
        keep(2 * level + 1, ratio_hi)
        excess = (
            excess
            + ratio_lo * roll_to(excess, stride, axis)
            + ratio_hi * roll_to(excess, -stride, axis)
        )
        link = ratio_lo * roll_to(link, stride, axis)
    return 1.0 / excess


def chain_solve(load, inverse, load_source, axis):
    source = load_source
    for level, stride in enumerate(levels_of(source.shape[axis])):
        source = (
            source
            + load(2 * level) * roll_to(source, stride, axis)
            + load(2 * level + 1) * roll_to(source, -stride, axis)
        )
    return source * inverse


def kernel(
    rows, cols,
    *refs,
):
    hbm = refs[:8]
    (
    o_ex, o_ey, o_ez, o_hx, o_hy, o_hz,
    y_mat, z_mat, y_mat_in, z_mat_in,
    y_src, z_src, y_src_in, z_src_in,
    y_out, z_out, y_back,
    face_z, halo_y, halo_z,
    y_alpha, y_beta, z_alpha, z_beta, z_fwd, z_bwd,
    x_fac, y_fac, z_fac,
    halo_sems, row_send, row_recv, col_send, col_recv,
    fields, field_sems,
    ) = refs[8:]
    ex, ey, ez, hx, hy, hz, eps, sig = [fields.at[i] for i in range(8)]
    loads = [
        pltpu.make_async_copy(hbm[i], fields.at[i], field_sems.at[i]) for i in range(8)
    ]
    for i in (6, 7, 0, 4, 2, 3, 5, 1):
        loads[i].start()
    ny, nz, nx = ex.shape
    r = lax.axis_index("row")
    c = lax.axis_index("col")
    zero_y = jnp.zeros(halo_y.shape, jnp.float32)
    zero_z = jnp.zeros(halo_z.shape, jnp.float32)
    halo_y[...] = zero_y
    halo_z[...] = zero_z
    barrier = pltpu.get_barrier_semaphore()
    for d in range(1, rows):
        pl.semaphore_signal(
            barrier, inc=1, device_id=(lax.rem(r + d, rows), c), device_id_type=MESH
        )
    for d in range(1, cols):
        pl.semaphore_signal(
            barrier, inc=1, device_id=(r, lax.rem(c + d, cols)), device_id_type=MESH
        )

    def halo(number, source, target, device):
        return pltpu.make_async_remote_copy(
            src_ref=source, dst_ref=target,
            send_sem=halo_sems.at[0, number], recv_sem=halo_sems.at[1, number],
            device_id=device, device_id_type=MESH,
        )

    low_r, high_r = jnp.maximum(r - 1, 0), jnp.minimum(r + 1, rows - 1)
    low_c, high_c = jnp.maximum(c - 1, 0), jnp.minimum(c + 1, cols - 1)
    halos = [
        (r > 0, r < rows - 1, halo(0, ez.at[0], halo_y.at[0], (low_r, c))),
        (c < cols - 1, c > 0, halo(1, face_z.at[1], halo_z.at[1], (r, high_c))),
        (r < rows - 1, r > 0, halo(2, hx.at[ny - 1], halo_y.at[1], (high_r, c))),
        (c > 0, c < cols - 1, halo(3, face_z.at[0], halo_z.at[0], (r, low_c))),
    ]

    def start_halos():
        for target, _, copy in halos:
            pl.when(target)(copy.start)

    def wait_halo(number):
        target, sender, copy = halos[number]
        pl.when(sender)(copy.wait_recv)

    sent = []

    def exchange(step, axis, source, target):
        if axis == "row":
            count, me, send, recv = rows, r, row_send, row_recv
        else:
            count, me, send, recv = cols, c, col_send, col_recv
        copies = []
        for d in range(1, count):
            peer = lax.rem(me + d, count)
            copies.append(
                pltpu.make_async_remote_copy(
                    src_ref=source.at[peer] if axis == "row" else source,
                    dst_ref=target.at[me],
                    send_sem=send.at[step, d - 1], recv_sem=recv.at[step, d - 1],
                    device_id=(peer, c) if axis == "row" else (r, peer),
                    device_id_type=MESH,
                )
            )
        for copy in copies:
            copy.start()
        target[me] = source[me] if axis == "row" else source[...]
        sent.extend(copies)
        return copies

    def arrive(copies):
        for copy in copies:
            copy.wait_recv()

    loads[6].wait()
    loads[7].wait()
    ground = (eps[...] + SIDE * sig[...]) * (1.0 / AREA)
    link = jnp.ones((nz, nx), jnp.float32)
    left = ground[0]
    carry = ground[1] * 0.0
    for j in range(1, ny):
        here = ground[j] + carry
        beta = 1.0 / (link + 1.0 + here)
        alpha = link * beta
        y_alpha[j] = alpha
        y_beta[j] = beta
        left = left + alpha * here
        carry = beta * here
        link = alpha
    for p in range(rows):
        y_mat[p, 0:1, :] = link[p : p + 1]
        y_mat[p, 1:2, :] = left[p : p + 1]
        y_mat[p, 2:3, :] = carry[p : p + 1]
    for i in (0, 4, 2, 3):
        loads[i].wait()
    face_z[0] = ex[:, 0:1, :]
    face_z[1] = hy[:, nz - 1 : nz, :]
    pl.semaphore_wait(barrier, rows - 1 + cols - 1)
    start_halos()
    y_mat_copies = exchange(0, "row", y_mat, y_mat_in)

    spot = lax.broadcasted_iota(jnp.int32, (ny, nz, nx), 1)
    here = ground
    link = jnp.ones((ny, nz, nx), jnp.float32)
    beta = jnp.ones((ny, nz, nx), jnp.float32)
    for j in range(1, nz):
        flow = beta * here if j > 1 else jnp.zeros_like(here)
        fresh_link = link if j == 1 else roll_to(link * beta, 1, 1)
        fresh = ground + roll_to(flow, 1, 1)
        here = jnp.where(spot == j, fresh, here)
        link = jnp.where(spot == j, fresh_link, link)
        beta = jnp.where(spot == j, 1.0 / (link + 1.0 + here), beta)
    first = spot == 0
    beta = jnp.where(first, 0.0, beta)
    alpha = link * beta
    z_alpha[...] = alpha
    z_beta[...] = beta
    left = jnp.sum(jnp.where(first, ground, alpha * here), axis=1)
    tail = beta * here
    z_mat[0] = alpha[:, nz - 1, :]
    z_mat[1] = left
    z_mat[2] = tail[:, nz - 1, :]
    z_mat_copies = exchange(0, "col", z_mat, z_mat_in)
    forward = jnp.where(first, 0.0, roll_to(beta, 1, 1))
    backward = jnp.where(spot == nz - 1, 0.0, beta)
    for level, stride in enumerate(levels_of(nz)):
        z_fwd[level] = forward
        z_bwd[level] = backward
        forward = forward * jnp.where(spot < stride, 0.0, roll_to(forward, stride, 1))
        backward = backward * jnp.where(
            spot >= nz - stride, 0.0, roll_to(backward, -stride, 1)
        )

    def reduce_y(body, flux):
        charge = []
        left = body[0] + flux[0]
        for j in range(1, ny):
            now = body[j] + flux[j] - flux[j - 1]
            if j > 1:
                now = now + y_beta[j - 1] * charge[-1]
            charge.append(now)
            left = left + y_alpha[j] * now
        right = y_beta[ny - 1] * charge[-1] - flux[ny - 1]
        return charge, left, right

    def send_y(stage, left, right):
        for p in range(rows):
            y_src[stage, p, 0:1, :] = left[p : p + 1]
            y_src[stage, p, 1:2, :] = right[p : p + 1]
        return exchange(1 + 2 * stage, "row", y_src.at[stage], y_src_in.at[stage])

    def expand_y(stage, charge):
        near = jnp.concatenate([y_back[stage, p, 0:1, :] for p in range(rows)], 0)
        beyond = jnp.concatenate([y_back[stage, p, 1:2, :] for p in range(rows)], 0)
        cells = []
        after = beyond
        for j in range(ny - 1, 0, -1):
            after = y_alpha[j] * near + y_beta[j] * (after + charge[j - 1])
            cells.insert(0, after)
        return jnp.stack([near] + cells, 0), beyond[None]

    def reduce_z(body, flux):
        source = body + flux - jnp.where(first, 0.0, roll_to(flux, 1, 1))
        charge = jnp.where(first, 0.0, source)
        for level, stride in enumerate(levels_of(nz)):
            charge = charge + z_fwd[level] * roll_to(charge, stride, 1)
        left = jnp.sum(jnp.where(first, source, z_alpha[...] * charge), axis=1)
        right = z_beta[...] * charge - flux
        return charge, left, right

    def send_z(stage, left, right):
        z_src[stage, 0] = left
        z_src[stage, 1] = right[:, nz - 1, :]
        return exchange(1 + 2 * stage, "col", z_src.at[stage], z_src_in.at[stage])

    def expand_z(stage, charge):
        near = z_out[stage, c][:, None, :]
        beyond = z_out[stage, c + 1][:, None, :]
        cells = z_alpha[...] * near + z_beta[...] * charge
        cells = cells + jnp.where(spot == nz - 1, z_beta[...] * beyond, 0.0)
        cells = jnp.where(first, near, cells)
        for level, stride in enumerate(levels_of(nz)):
            cells = cells + z_bwd[level] * roll_to(cells, -stride, 1)
        return cells, beyond

    tall = 8

    def rows_of(buffer, number, count, filler):
        parts = [buffer[p, number : number + 1, :] for p in range(count)]
        if count < tall:
            parts.append(jnp.full((tall - count, nx), filler, jnp.float32))
        return jnp.concatenate(parts, 0)

    def line_factors(buffer, count, keep):
        row = lax.broadcasted_iota(jnp.int32, (tall, nx), 0)
        link = rows_of(buffer, 0, count, 0.0)
        left = rows_of(buffer, 1, count, 1.0)
        right = rows_of(buffer, 2, count, 0.0)
        below = row == 0
        excess = left + jnp.where(below, 0.0, roll_to(right, 1, 0))
        excess = excess + jnp.where(row == count - 1, link, 0.0)
        inner_link = jnp.where(below | (row >= count), 0.0, roll_to(link, 1, 0))
        return chain_factors(inner_link, excess, 0, keep)

    def line_solve(stage, source_in, count, load, inverse, out):
        row = lax.broadcasted_iota(jnp.int32, (tall, nx), 0)
        left = rows_of(source_in.at[stage], 0, count, 0.0)
        right = rows_of(source_in.at[stage], 1, count, 0.0)
        source = left + jnp.where(row == 0, 0.0, roll_to(right, 1, 0))
        source = jnp.where(row < count, source, 0.0)
        near = chain_solve(load, inverse, source, 0)
        for p in range(count):
            out[stage, p, 0:1, :] = near[p : p + 1]
            if p < count - 1:
                out[stage, p, 1:2, :] = near[p + 1 : p + 2]
            else:
                out[stage, p, 1:2, :] = jnp.zeros((1, nx), jnp.float32)

    def keeper(ref):
        def keep(number, values):
            ref[number] = values
        return keep

    def loader(ref):
        def load(number):
            return ref[number]
        return load

    first_x = lax.broadcasted_iota(jnp.int32, (ny, nz, nx), 2) == 0
    last_x = lax.broadcasted_iota(jnp.int32, (ny, nz, nx), 2) == nx - 1
    x_inverse = chain_factors(
        jnp.where(first_x, 0.0, 1.0), ground + jnp.where(last_x, 1.0, 0.0), 2, keeper(x_fac)
    )

    loads[5].wait()
    loads[1].wait()
    keep_ground = (eps[...] - SIDE * sig[...]) * (1.0 / AREA)
    flux_of_z = hz[...] * (1.0 / STEP) - up_x(ey[...])
    wait_halo(1)
    body = keep_ground * ex[...] - down_z(hy[...], halo_z[1]) * (1.0 / STEP)
    y_charge, left, right = reduce_y(body, flux_of_z)
    y_copies = send_y(0, left, right)
    wait_halo(0)
    flux_of_x = hx[...] * (1.0 / STEP) - up_y(ez[...], halo_y[0:1])
    body = keep_ground * ey[...] - down_x(hz[...]) * (1.0 / STEP)
    z_charge, left, right = reduce_z(body, flux_of_x)
    z_copies = send_z(0, left, right)

    wait_halo(2)
    wait_halo(3)
    flux_of_y = hy[...] * (1.0 / STEP) - up_z(ex[...], halo_z[0])
    body = keep_ground * ez[...] - down_y(hx[...], halo_y[1:2]) * (1.0 / STEP)
    half_ez = chain_solve(loader(x_fac), x_inverse, body + down_x(flux_of_y), 2)
    slope_ez = up_x(half_ez)

    arrive(y_mat_copies)
    y_inverse = line_factors(y_mat_in, rows, keeper(y_fac))
    arrive(z_mat_copies)
    grounded = z_mat_in[0, 1]
    for q in range(cols):
        link = z_mat_in[q, 0]
        inverse = 1.0 / (grounded + link)
        z_fac[0, q] = link * inverse
        z_fac[1, q] = inverse
        if q < cols - 1:
            grounded = z_mat_in[q + 1, 1] + z_mat_in[q, 2] + link * inverse * grounded

    def half_lines(stage, y_copies, z_copies, between):
        arrive(y_copies)
        line_solve(stage, y_src_in, rows, loader(y_fac), y_inverse, y_out)
        y_returns = exchange(2 + 2 * stage, "row", y_out.at[stage], y_back.at[stage])
        between()
        arrive(z_copies)
        source = [z_src_in[stage, 0, 0]]
        for q in range(1, cols):
            own = z_src_in[stage, q, 0] + z_src_in[stage, q - 1, 1]
            source.append(own + z_fac[0, q - 1] * source[-1])
        value = jnp.zeros((ny, nx), jnp.float32)
        z_out[stage, cols] = value
        for q in range(cols - 1, -1, -1):
            value = z_fac[1, q] * source[q] + z_fac[0, q] * value
            z_out[stage, q] = value
        return y_returns

    y_returns = half_lines(0, y_copies, z_copies, lambda: None)

    half_ey, beyond_ey = expand_z(0, z_charge)
    slope_ey = up_z(half_ey, beyond_ey)

    lossless = eps[...] * (1.0 / AREA)
    lossy = sig[...] * (SIDE / AREA)
    late_charge, left, right = reduce_y(lossless * half_ez + lossy * ez[...], -slope_ey)
    y_copies = send_y(1, left, right)
    arrive(y_returns)
    half_ex, beyond_ex = expand_y(0, y_charge)
    slope_ex = up_y(half_ex, beyond_ex)
    z_charge, left, right = reduce_z(lossless * half_ex + lossy * ex[...], -slope_ez)
    z_copies = send_z(1, left, right)

    def solve_ey():
        body = lossless * half_ey + lossy * ey[...]
        mean_ey = chain_solve(loader(x_fac), x_inverse, body - down_x(slope_ex), 2)
        next_ey = 2.0 * mean_ey - ey[...]
        o_ey[...] = next_ey
        o_hz[...] = STEP * (flux_of_z + 2.0 * slope_ex - up_x(next_ey))

    y_returns = half_lines(1, y_copies, z_copies, solve_ey)
    arrive(y_returns)
    mean_ez, beyond_ez = expand_y(1, late_charge)
    next_ez = 2.0 * mean_ez - ez[...]
    o_ez[...] = next_ez
    above = 2.0 * beyond_ez - halo_y[0:1]
    o_hx[...] = STEP * (flux_of_x + 2.0 * slope_ey - up_y(next_ez, above))
    mean_ex, beyond_ex = expand_z(1, z_charge)
    next_ex = 2.0 * mean_ex - ex[...]
    o_ex[...] = next_ex
    above = 2.0 * beyond_ex - halo_z[0]
    o_hy[...] = STEP * (flux_of_y + 2.0 * slope_ez - up_z(next_ex, above))

    for target, _, copy in halos:
        pl.when(target)(copy.wait_send)
    for copy in sent:
        copy.wait_send()


def deliver(*refs):
    held, results, sems = refs[:6], refs[6:12], refs[12]
    copies = [
        pltpu.make_async_copy(held[i], results[i], sems.at[i]) for i in range(6)
    ]
    for copy in copies:
        copy.start()
    for copy in copies:
        copy.wait()


def fused(rows, cols, *fields):
    ny, nz, nx = fields[0].shape
    f32 = jnp.float32
    block = (ny, nz, nx)
    y_levels = len(levels_of(8))
    scratch = [
        (rows, 3, nx), (3, ny, nx), (rows, 3, nx), (cols, 3, ny, nx),
        (2, rows, 2, nx), (2, 2, ny, nx), (2, rows, 2, nx), (2, cols, 2, ny, nx),
        (2, rows, 2, nx), (2, cols + 1, ny, nx), (2, rows, 2, nx),
        (2, ny, 1, nx), (2, nz, nx), (2, ny, 1, nx),
        block, block, block, block,
        (len(levels_of(nz)),) + block, (len(levels_of(nz)),) + block,
        (2 * len(levels_of(nx)),) + block, (2 * y_levels, 8, nx), (2, cols, ny, nx),
    ]
    held = pl.pallas_call(
        functools.partial(kernel, rows, cols),
        out_shape=[pltpu.VMEM(block, f32)] * 6,
        in_specs=[pl.BlockSpec(memory_space=pl.ANY)] * 8,
        out_specs=[pl.BlockSpec(memory_space=pltpu.VMEM)] * 6,
        scratch_shapes=[pltpu.VMEM(shape, f32) for shape in scratch]
        + [
            pltpu.SemaphoreType.DMA((2, 4)),
            pltpu.SemaphoreType.DMA((5, rows - 1)),
            pltpu.SemaphoreType.DMA((5, rows - 1)),
            pltpu.SemaphoreType.DMA((5, cols - 1)),
            pltpu.SemaphoreType.DMA((5, cols - 1)),
            pltpu.VMEM((8,) + block, f32),
            pltpu.SemaphoreType.DMA((8,)),
        ],
        compiler_params=pltpu.CompilerParams(
            collective_id=0, has_side_effects=True, vmem_limit_bytes=VMEM_LIMIT
        ),
        name="step",
    )(*[pltpu.with_memory_space_constraint(field, pltpu.HBM) for field in fields])
    return pl.pallas_call(
        deliver,
        out_shape=[jax.ShapeDtypeStruct(block, f32)] * 6,
        in_specs=[pl.BlockSpec(memory_space=pltpu.VMEM)] * 6,
        out_specs=[pl.BlockSpec(memory_space=pl.ANY)] * 6,
        scratch_shapes=[pltpu.SemaphoreType.DMA((6,))],
        compiler_params=pltpu.CompilerParams(vmem_limit_bytes=1024 * 1024),
        name="deliver",
    )(*held)


HALF_STEP = 30.0


def with_halo(cells, sides, width):
    for axis, dim in sides:
        count = lax.axis_size(axis)
        ends = count - 1
        head = lax.slice_in_dim(cells, 0, width, axis=dim)
        tail = lax.slice_in_dim(cells, cells.shape[dim] - width, cells.shape[dim], axis=dim)
        cells = jnp.concatenate(
            [
                lax.ppermute(tail, axis, [(i, (i + 1) % count) for i in range(ends)]),
                cells,
                lax.ppermute(head, axis, [((i + 1) % count, i) for i in range(ends)]),
            ],
            axis=dim,
        )
    return cells


def shifted(values, stride, line_axis, filler, forward):
    length = values.shape[line_axis]
    padding = jnp.full_like(lax.slice_in_dim(values, 0, stride, axis=line_axis), filler)
    if forward:
        return jnp.concatenate(
            [lax.slice_in_dim(values, stride, length, axis=line_axis), padding], line_axis
        )
    return jnp.concatenate(
        [padding, lax.slice_in_dim(values, 0, length - stride, axis=line_axis)], line_axis
    )


def diff_up(values, line_axis):
    return shifted(values, 1, line_axis, 0.0, True) - values


def diff_down(values, line_axis):
    return values - shifted(values, 1, line_axis, 0.0, False)


def reduce_lines(sub_diag, main_diag, super_diag, source, line_axis):
    length = source.shape[line_axis]
    stride = 1
    while stride < length:
        sub_lo = shifted(sub_diag, stride, line_axis, 0.0, False)
        mid_lo = shifted(main_diag, stride, line_axis, 1.0, False)
        sup_lo = shifted(super_diag, stride, line_axis, 0.0, False)
        src_lo = shifted(source, stride, line_axis, 0.0, False)
        sub_hi = shifted(sub_diag, stride, line_axis, 0.0, True)
        mid_hi = shifted(main_diag, stride, line_axis, 1.0, True)
        sup_hi = shifted(super_diag, stride, line_axis, 0.0, True)
        src_hi = shifted(source, stride, line_axis, 0.0, True)
        ratio_lo = sub_diag / mid_lo
        ratio_hi = super_diag / mid_hi
        sub_diag = -sub_lo * ratio_lo
        super_diag = -sup_hi * ratio_hi
        main_diag = main_diag - sup_lo * ratio_lo - sub_hi * ratio_hi
        source = source - src_lo * ratio_lo - src_hi * ratio_hi
        stride = stride * 2
    return source / main_diag


def line_flags(length, line_axis, rank):
    iota_shape = [1] * rank
    iota_shape[line_axis] = length
    where_line = lax.broadcasted_iota(jnp.int32, tuple(iota_shape), line_axis)
    return (where_line == 0, where_line == length - 1)


def line_system(coupling, is_first, is_final):
    sub_diag = jnp.where(is_first, 0.0, -coupling)
    main_diag = jnp.where(is_first, 1.0 + coupling, 1.0 + 2.0 * coupling)
    super_diag = jnp.where(is_final, 0.0, -coupling)
    return (sub_diag, main_diag, super_diag)


def solve_local(source, coupling, line_axis):
    is_first, is_final = line_flags(source.shape[line_axis], line_axis, source.ndim)
    sub_diag, main_diag, super_diag = line_system(coupling, is_first, is_final)
    return reduce_lines(sub_diag, main_diag, super_diag, source, line_axis)


def inner(values):
    return values[1:-1, 1:-1]


def with_faces(stacked):
    return with_halo(stacked, (("row", 1), ("col", 2)), 1)


def inside_mask(count_y, count_z):
    pos_y = (
        lax.axis_index("row") * count_y
        + lax.broadcasted_iota(jnp.int32, (count_y + 2, 1, 1), 0)
        - 1
    )
    pos_z = (
        lax.axis_index("col") * count_z
        + lax.broadcasted_iota(jnp.int32, (1, count_z + 2, 1), 1)
        - 1
    )
    inside = (
        (pos_y >= 0)
        & (pos_y < count_y * lax.axis_size("row"))
        & (pos_z >= 0)
        & (pos_z < count_z * lax.axis_size("col"))
    )
    return inside.astype(jnp.float32)


def solve_rows_moved(source, coupling):

    def along_lines(pieces):
        moved_source, moved_coupling = pieces
        turned_source = jnp.transpose(moved_source, (1, 2, 0))
        turned_coupling = jnp.transpose(moved_coupling, (1, 2, 0))
        solved = solve_local(turned_source, turned_coupling, 2)
        solved = jnp.transpose(solved, (2, 0, 1))
        return lax.all_to_all(solved, "row", split_axis=0, concat_axis=2, tiled=True)

    return along_lines(
        (
            lax.all_to_all(source, "row", split_axis=2, concat_axis=0, tiled=True),
            lax.all_to_all(coupling, "row", split_axis=2, concat_axis=0, tiled=True),
        )
    )


def solve_rows(source, coupling):
    return solve_rows_moved(source, coupling)


def solve_columns(source, coupling):

    def along_lines(pieces):
        moved_source, moved_coupling = pieces
        solved = solve_local(moved_source, moved_coupling, 1)
        return lax.all_to_all(solved, "col", split_axis=1, concat_axis=2, tiled=True)

    return along_lines(
        (
            lax.all_to_all(source, "col", split_axis=2, concat_axis=1, tiled=True),
            lax.all_to_all(coupling, "col", split_axis=2, concat_axis=1, tiled=True),
        )
    )


def on_device(
    efield_x, efield_y, efield_z, hfield_x, hfield_y, hfield_z, permittivity, conductivity
):
    count_y = efield_x.shape[0]
    count_z = efield_x.shape[1]
    damping = conductivity * HALF_STEP / (2.0 * permittivity)
    keep_coef = (1.0 - damping) / (1.0 + damping)
    drive_coef = HALF_STEP / (permittivity * (1.0 + damping))
    coupling = drive_coef * HALF_STEP
    old_all = with_faces(jnp.stack([efield_x, efield_y, efield_z, hfield_x, hfield_y, hfield_z]))
    old_ex, old_ey, old_ez = (old_all[0], old_all[1], old_all[2])
    old_hx, old_hy, old_hz = (old_all[3], old_all[4], old_all[5])
    source_x = keep_coef * efield_x + drive_coef * (
        inner(diff_down(old_hz, 0))
        - inner(diff_down(old_hy, 1))
        - HALF_STEP * inner(diff_down(diff_up(old_ey, 2), 0))
    )
    source_y = keep_coef * efield_y + drive_coef * (
        inner(diff_down(old_hx, 1))
        - diff_down(hfield_z, 2)
        - HALF_STEP * inner(diff_down(diff_up(old_ez, 0), 1))
    )
    source_z = keep_coef * efield_z + drive_coef * (
        diff_down(hfield_y, 2)
        - inner(diff_down(old_hx, 0))
        - HALF_STEP * inner(diff_down(diff_up(old_ex, 1), 2))
    )
    half_ex = solve_rows(source_x, coupling)
    half_ey = solve_columns(source_y, coupling)
    half_ez = solve_local(source_z, coupling, 2)
    mid_all = with_faces(jnp.stack([half_ex, half_ey, half_ez]))
    mid_ex, mid_ey, mid_ez = (mid_all[0], mid_all[1], mid_all[2])
    inside = inside_mask(count_y, count_z)
    dz_mid_ey = diff_up(mid_ey, 1)
    dx_mid_ez = diff_up(mid_ez, 2)
    dy_mid_ex = diff_up(mid_ex, 0)
    mid_hx = (old_hx + HALF_STEP * (dz_mid_ey - diff_up(old_ez, 0))) * inside
    mid_hy = (old_hy + HALF_STEP * (dx_mid_ez - diff_up(old_ex, 1))) * inside
    mid_hz = (old_hz + HALF_STEP * (dy_mid_ex - diff_up(old_ey, 2))) * inside
    second_x = keep_coef * half_ex + drive_coef * (
        inner(diff_down(mid_hz, 0))
        - inner(diff_down(mid_hy, 1))
        - HALF_STEP * inner(diff_down(dx_mid_ez, 1))
    )
    second_y = keep_coef * half_ey + drive_coef * (
        inner(diff_down(mid_hx, 1))
        - inner(diff_down(mid_hz, 2))
        - HALF_STEP * inner(diff_down(dy_mid_ex, 2))
    )
    second_z = keep_coef * half_ez + drive_coef * (
        inner(diff_down(mid_hy, 2))
        - inner(diff_down(mid_hx, 0))
        - HALF_STEP * inner(diff_down(dz_mid_ey, 0))
    )
    next_ex = solve_columns(second_x, coupling)
    next_ey = solve_local(second_y, coupling, 2)
    next_ez = solve_rows(second_z, coupling)
    last_all = with_faces(jnp.stack([next_ex, next_ez]))
    next_hx = inner(mid_hx) + HALF_STEP * (inner(dz_mid_ey) - inner(diff_up(last_all[1], 0)))
    next_hy = inner(mid_hy) + HALF_STEP * (inner(dx_mid_ez) - inner(diff_up(last_all[0], 1)))
    next_hz = inner(mid_hz) + HALF_STEP * (inner(dy_mid_ex) - diff_up(next_ey, 2))
    return (next_ex, next_ey, next_ez, next_hx, next_hy, next_hz)


def solution(mesh):
    rows, cols = mesh.shape["row"], mesh.shape["col"]
    placed = (
        P("row", "col", None),
        P("row", "col", None),
        P("row", "col", None),
        P("row", "col", None),
        P("row", "col", None),
        P("row", "col", None),
        P("row", "col", None),
        P("row", "col", None),
    )

    def per_device(*fields):
        ny, nz = fields[0].shape[:2]
        if nz == rows == 8 and ny == cols and 1 < cols < 8:
            return tuple(fused(rows, cols, *fields))
        return on_device(*fields)

    return jax.shard_map(
        per_device,
        mesh=mesh,
        in_specs=placed,
        out_specs=(
            P("row", "col", None),
            P("row", "col", None),
            P("row", "col", None),
            P("row", "col", None),
            P("row", "col", None),
            P("row", "col", None),
        ),
        check_vma=False,
    )
```
